512 devices in a mesh: dp: 512 (over y, z, x, core).
Axes of the slice: x: 4, y: 4, z: 16, core: 2. Of those that a mesh axis runs over, the one named last changes fastest.
Arguments:
- img_feat: bfloat16 [131072, 1152], P('dp'), may hold values from -6 to 6
- head_weight: bfloat16 [1152, 640], replicated, may hold values from -0.1875 to 0.1875
- txt_emb: bfloat16 [131072, 640], P('dp'), may hold values from -6 to 6
- labels: int32 [131072], P('dp'), may hold values from 0 to 63
- log_logit_scale: float32 [1], replicated, may hold values from 0 to 1.5
- bias: float32 [1], replicated, may hold values from -3 to -1
Outputs:
- d_img_feat: bfloat16 [131072, 1152], P('dp')
- d_txt_emb: bfloat16 [131072, 640], P('dp')
- d_head: bfloat16 [1152, 640], replicated
The draws below stay inside these ranges and needn't reach their ends.
All inputs are finite; a program needn't handle non-finite values.
Results may differ from the reference program's by a relative error of at most 0.0065.
Values may be sent and summed in bfloat16 or wider, within the bound.
No kernel may reach another device: no remote copies, remote signals or barrier semaphores. Data moves between devices by JAX's collectives and lax.ppermute only.
A program may use at most 64 MiB of HBM per device.

```python
import jax
import jax.numpy as jnp
from jax import lax

D = 1152
E = 640
TOK_DEV = 256
N = 131072
N_DP = 512


def place_ends(array, rng, smallest, top_value):
    longest = array.shape.index(max(array.shape))
    spots = []
    for shift in (0, 1):
        where = [jax.random.randint(jax.random.fold_in(rng, axis), (), 0, length) for axis, length in enumerate(array.shape)]
        where[longest] = (where[longest] + shift) % array.shape[longest]
        spots.append(tuple(where))
    return array.at[spots[0]].set(smallest).at[spots[1]].set(top_value)


def block_scale(key, shape, cuts, least, top_value):
    loudness = 1.0
    for position, blocks in cuts:
        steps = jax.random.uniform(jax.random.fold_in(jax.random.fold_in(key, 6), position), (blocks,), jnp.float32, least / len(cuts), top_value / len(cuts))
        loudness = loudness * jnp.repeat(jnp.exp(steps), shape[position] // blocks).reshape((-1,) + (1,) * (len(shape) - 1 - position))
    return loudness


def centred(rng, dims, spread, limit, pieces=(), held_as=jnp.bfloat16):
    values = spread * jax.random.normal(rng, dims, jnp.float32)
    if pieces:
        values = values * block_scale(rng, dims, pieces, -0.22, 0.18)
    return jnp.clip(values, -limit, limit).astype(held_as)


def setup_inputs(seed: int = 0) -> dict:
    seeds = jax.random.split(jax.random.key(seed), 7)
    return {
        "img_feat": centred(seeds[0], (N, D), 1.0, 6.0, ((0, 512),)),
        "head_weight": centred(seeds[1], (D, E), D ** -0.5, 0.1875),
        "txt_emb": centred(seeds[2], (N, E), 1.0, 6.0, ((0, 512),)),
        "labels": place_ends(jax.random.randint(seeds[3], (N,), 0, TOK_DEV // 4), jax.random.fold_in(seeds[3], 1), 0, (TOK_DEV // 4) - 1).astype(jnp.int32),
        "log_logit_scale": jnp.clip(jax.random.uniform(seeds[4], (1,), jnp.float32, 0.0, 1.5), 0.0, 1.5),
        "bias": jnp.clip(jax.random.uniform(seeds[5], (1,), jnp.float32, -3.0, -1.0), -3.0, -1.0),
    }


def reference(img_feat, head_weight, txt_emb, labels, log_logit_scale, bias):
    proj = jnp.dot(img_feat, head_weight, preferred_element_type=jnp.float32)
    inv_img = lax.rsqrt(lax.optimization_barrier(jnp.sum(proj * proj, axis=-1, keepdims=True)) + 1e-06)
    unit_img = proj * inv_img
    image_unit_rows = unit_img.astype(jnp.bfloat16)
    txt_float = txt_emb.astype(jnp.float32)
    inv_txt = lax.rsqrt(lax.optimization_barrier(jnp.sum(txt_float * txt_float, axis=-1, keepdims=True)) + 1e-06)
    unit_txt = txt_float * inv_txt
    text_unit_rows = unit_txt.astype(jnp.bfloat16)
    logit_scale_value = jnp.exp(log_logit_scale[0])
    logit_bias_value = bias[0]
    block_count = N_DP
    img_blocks = image_unit_rows.reshape(block_count, TOK_DEV, E)
    txt_blocks = text_unit_rows.reshape(block_count, TOK_DEV, E)
    label_blocks = labels.reshape(block_count, TOK_DEV)

    def step_block(text_grads, block_index):
        local_images = img_blocks[block_index]
        image_gradient = jnp.zeros((TOK_DEV, E), jnp.float32)
        for round_code in (0, 1, 3, 7, 15):
            partner = jnp.bitwise_xor(block_index, round_code).astype(jnp.int32)
            partner_captions = txt_blocks[partner]
            pair_logits = logit_scale_value * lax.dot_general(local_images, partner_captions, (((1,), (1,)), ((), ())), preferred_element_type=jnp.float32) + logit_bias_value
            if round_code == 0:
                block_labels = label_blocks[block_index]
                label_sign_value = jnp.where(block_labels[:, None] == block_labels[None, :], 1.0, -1.0).astype(jnp.float32)
            else:
                label_sign_value = -jnp.ones_like(pair_logits)
            block_gradient = (-label_sign_value * jax.nn.sigmoid(-label_sign_value * pair_logits)).astype(jnp.bfloat16)
            image_gradient = image_gradient + logit_scale_value * jnp.dot(block_gradient, partner_captions, preferred_element_type=jnp.float32)
            partner_gradient = logit_scale_value * lax.dot_general(block_gradient, local_images, (((0,), (0,)), ((), ())), preferred_element_type=jnp.float32)
            text_grads = text_grads.at[partner].add(partner_gradient)
        return (text_grads, image_gradient)
    text_grads, unit_image_gradient = lax.scan(step_block, jnp.zeros((block_count, TOK_DEV, E), jnp.float32), jnp.arange(block_count, dtype=jnp.int32))
    unit_image_gradient = unit_image_gradient.reshape(N, E)
    unit_text_gradient = text_grads.reshape(N, E)
    d_proj = ((unit_image_gradient - unit_img * lax.optimization_barrier(jnp.sum(unit_img * unit_image_gradient, axis=-1, keepdims=True))) * inv_img).astype(jnp.bfloat16)
    d_head = lax.dot_general(img_feat, d_proj, (((0,), (0,)), ((), ())), preferred_element_type=jnp.float32).astype(jnp.bfloat16)
    d_img_feat = lax.dot_general(d_proj, head_weight, (((1,), (1,)), ((), ())), preferred_element_type=jnp.float32).astype(jnp.bfloat16)
    d_txt_emb = ((unit_text_gradient - unit_txt * lax.optimization_barrier(jnp.sum(unit_txt * unit_text_gradient, axis=-1, keepdims=True))) * inv_txt).astype(jnp.bfloat16)
    return (d_img_feat, d_txt_emb, d_head)
```

```python
import jax
import jax.numpy as jnp
from jax import lax
from jax.experimental import pallas as pl
from jax.experimental.pallas import tpu as pltpu
from jax.sharding import PartitionSpec as P

ROUNDS = (1, 3, 7, 15)
F32 = jnp.float32
BF16 = jnp.bfloat16


def swap(value, mask):
    pairs = [(source, source ^ mask) for source in range(lax.axis_size("dp"))]
    return lax.ppermute(value, "dp", pairs)


def after(value, *others):
    return lax.optimization_barrier((value,) + others)[0]


def rows_dot(left, right):
    return lax.dot_general(left, right, (((1,), (1,)), ((), ())), preferred_element_type=F32)


def part(value, start, size):
    return lax.dynamic_slice_in_dim(value, start, size, 0)


def head_kernel(label_ref, feat_ref, d_proj_ref, sent_ref, kept_ref):
    label = label_ref[0]
    for b in range(9):
        product = lax.dot_general(
            feat_ref[:, 128 * b : 128 * b + 128],
            d_proj_ref[...],
            (((0,), (0,)), ((), ())),
            preferred_element_type=F32,
        )
        for a in range(8):
            slab = product[16 * a : 16 * a + 16]
            chunk = label ^ a

            @pl.when(chunk >= 4)
            def _():
                sent_ref[chunk - 4, b] = slab.astype(BF16)

            @pl.when(chunk < 4)
            def _():
                kept_ref[chunk, b] = slab


def head_terms(label, feat, d_proj):
    return pl.pallas_call(
        head_kernel,
        out_shape=(
            jax.ShapeDtypeStruct((4, 9, 16, 640), BF16),
            jax.ShapeDtypeStruct((4, 9, 16, 640), F32),
        ),
        in_specs=[
            pl.BlockSpec(memory_space=pltpu.SMEM),
            pl.BlockSpec(memory_space=pltpu.VMEM),
            pl.BlockSpec(memory_space=pltpu.VMEM),
        ],
        out_specs=(
            pl.BlockSpec(memory_space=pltpu.VMEM),
            pl.BlockSpec(memory_space=pltpu.VMEM),
        ),
        compiler_params=pltpu.CompilerParams(vmem_limit_bytes=32 << 20),
        cost_estimate=pl.CostEstimate(flops=377487360, bytes_accessed=4000000, transcendentals=0),
    )(label, feat, d_proj)


def place_kernel(label_ref, mine_ref, other_ref, out_ref, sems):
    label = label_ref[0]
    copies = []
    for k in range(8):
        source = mine_ref.at[k] if k < 4 else other_ref.at[k - 4]
        copies.append(pltpu.make_async_copy(source, out_ref.at[:, label ^ k], sems.at[k]))
    for copy in copies:
        copy.start()
    for copy in copies:
        copy.wait()


def place(label, mine, other):
    return pl.pallas_call(
        place_kernel,
        out_shape=jax.ShapeDtypeStruct((9, 8, 16, 640), BF16),
        in_specs=[
            pl.BlockSpec(memory_space=pltpu.SMEM),
            pl.BlockSpec(memory_space=pl.ANY),
            pl.BlockSpec(memory_space=pl.ANY),
        ],
        out_specs=pl.BlockSpec(memory_space=pl.ANY),
        scratch_shapes=[pltpu.SemaphoreType.DMA((8,))],
        cost_estimate=pl.CostEstimate(flops=0, bytes_accessed=3000000, transcendentals=0),
    )(label, mine, other)


def halve(kept, sent, mask):
    total = kept + swap(sent, mask).astype(F32)
    half = total.shape[0] // 2
    return total[:half], total[half:].astype(BF16)


def join(mine, mask):
    return jnp.concatenate([mine, swap(mine, mask)], axis=0)


def join_in_order(mine, mask, bit, overlap=0):
    other = swap(mine, mask)
    low = jnp.concatenate([mine, other[overlap:]], axis=0)
    high = jnp.concatenate([other, mine[overlap:]], axis=0)
    return jnp.where(bit == 1, high, low)


def per_device(img_feat, head_weight, txt_emb, labels, log_logit_scale, bias):
    index = lax.axis_index("dp")
    bits = [(index >> k) & 1 for k in range(9)]

    txt_float = txt_emb.astype(F32)
    inv_txt = lax.rsqrt(jnp.sum(txt_float * txt_float, axis=-1, keepdims=True) + 1e-06)
    unit_txt = txt_float * inv_txt
    txt_rows = unit_txt.astype(BF16)
    captions = {c: swap(txt_rows, c) for c in reversed(ROUNDS)}

    proj = jnp.dot(img_feat, head_weight, preferred_element_type=F32)
    inv_img = lax.rsqrt(jnp.sum(proj * proj, axis=-1, keepdims=True) + 1e-06)
    unit_img = proj * inv_img
    img_rows = unit_img.astype(BF16)
    scale = jnp.exp(log_logit_scale[0])
    shift = bias[0]

    sign = jnp.where(labels[:, None] == labels[None, :], 1.0, -1.0).astype(F32)
    logits = scale * rows_dot(img_rows, txt_rows) + shift
    grad = (-sign * jax.nn.sigmoid(-sign * logits)).astype(BF16)
    d_unit_img = jnp.dot(grad, txt_rows, preferred_element_type=F32)
    for c in ROUNDS:
        logits = scale * rows_dot(img_rows, captions[c]) + shift
        grad_c = jax.nn.sigmoid(logits).astype(BF16)
        d_unit_img = d_unit_img + jnp.dot(grad_c, captions[c], preferred_element_type=F32)
    d_unit_img = scale * d_unit_img
    d_proj = (
        (d_unit_img - unit_img * jnp.sum(unit_img * d_unit_img, axis=-1, keepdims=True)) * inv_img
    ).astype(BF16)

    x_low, x_high = bits[1] ^ bits[2], bits[2]
    y_low, y_high = bits[7] ^ bits[8], bits[8]
    label = (bits[0] * 4 + x_low * 2 + x_high)[None]
    sent, kept = head_terms(label, img_feat, d_proj)
    kept, sent = halve(kept, sent, 1)
    kept, sent = halve(kept, sent, 2)
    total = (kept + swap(sent, 6).astype(F32)).reshape(144, 640)
    sent = part(total, (1 - y_low) * 72, 72).astype(BF16)
    total = part(total, y_low * 72, 72) + swap(sent, 128).astype(F32)
    img_late = after(img_rows, total)
    images = {c: swap(img_late, c) for c in ROUNDS}
    sent = part(total, (1 - y_high) * 32, 40).astype(BF16)
    total = part(total, y_high * 32, 40) + swap(sent, 384).astype(F32)
    for z in (1, 2, 4, 15):
        mine = total.astype(BF16)
        total = mine.astype(F32) + swap(mine, z * 8).astype(F32)
    piece = join_in_order(total.astype(BF16), 384, y_high, 8)
    piece = join_in_order(piece, 128, y_low).reshape(1, 9, 16, 640)
    piece = after(piece, *images.values())
    piece = join(piece, 6)
    piece = join(piece, 2)
    d_head = place(label, piece, swap(piece, 1)).reshape(1152, 640)

    d_img_feat = rows_dot(d_proj, head_weight).astype(BF16)

    d_unit_txt = lax.dot_general(grad, img_rows, (((0,), (0,)), ((), ())), preferred_element_type=F32)
    for c in ROUNDS:
        logits = scale * rows_dot(txt_rows, images[c]) + shift
        grad_c = jax.nn.sigmoid(logits).astype(BF16)
        d_unit_txt = d_unit_txt + jnp.dot(grad_c, images[c], preferred_element_type=F32)
    d_unit_txt = scale * d_unit_txt
    d_txt_emb = (
        (d_unit_txt - unit_txt * jnp.sum(unit_txt * d_unit_txt, axis=-1, keepdims=True)) * inv_txt
    ).astype(BF16)
    return (d_img_feat, d_txt_emb, d_head)


def solution(mesh):
    return jax.shard_map(
        per_device,
        mesh=mesh,
        in_specs=(P("dp", None), P(), P("dp", None), P("dp"), P(), P()),
        out_specs=(P("dp", None), P("dp", None), P()),
        check_vma=False,
    )
```

```python
import jax
import jax.numpy as jnp
from jax import lax
from jax.experimental import pallas as pl
from jax.experimental.pallas import tpu as pltpu
from jax.sharding import PartitionSpec as P

D = 1152
E = 640
ROWS = 256
F32 = jnp.float32
BF16 = jnp.bfloat16
OWNERS, SLABS = 16, 12
SMEM = pl.BlockSpec(memory_space=pltpu.SMEM)
VMEM = pl.BlockSpec(memory_space=pltpu.VMEM)


def group(bits):
    mask = sum(1 << b for b in bits)
    members = [
        sum((k >> j & 1) << b for j, b in enumerate(bits)) for k in range(1 << len(bits))
    ]
    return [[base | m for m in members] for base in range(512) if not base & mask]


PLANE = group((1, 2, 7, 8))


def swap(value, mask):
    pairs = [(source, source ^ mask) for source in range(lax.axis_size("dp"))]
    return lax.ppermute(value, "dp", pairs)


def exchange(value):
    return lax.all_to_all(value, "dp", 0, 0, axis_index_groups=PLANE, tiled=True)


def after(value, *others):
    return lax.optimization_barrier((value,) + others)[0]


def shape(*dims, dtype=F32):
    return jax.ShapeDtypeStruct(dims, dtype)


def dot(left, right, left_dim=1, right_dim=0):
    return lax.dot_general(
        left, right, (((left_dim,), (right_dim,)), ((), ())), preferred_element_type=F32
    )


def call(kernel, out_shape, specs, flops, *operands, scratch=(), out_specs=None):
    return pl.pallas_call(
        kernel,
        out_shape=out_shape,
        in_specs=specs,
        out_specs=out_specs if out_specs is not None else jax.tree.map(lambda _: VMEM, out_shape),
        scratch_shapes=scratch,
        compiler_params=pltpu.CompilerParams(vmem_limit_bytes=32 << 20),
        cost_estimate=pl.CostEstimate(flops=flops, bytes_accessed=100000, transcendentals=0),
    )(*operands)


def inverse_norm(value):
    return lax.rsqrt(jnp.sum(value * value, axis=-1, keepdims=True) + 1e-06)


def tangent(d_unit, unit, inverse):
    return ((d_unit - unit * jnp.sum(unit * d_unit, axis=-1, keepdims=True)) * inverse).astype(BF16)


def text_kernel(core_ref, txt_ref, feat_ref, rows_ref, packed_ref):
    value = txt_ref[...].astype(F32)
    rows = (value * inverse_norm(value)).astype(BF16)
    rows_ref[...] = rows
    packed_ref[:, :E] = rows
    start = pl.multiple_of(512 * (1 - core_ref[0]), 128)
    packed_ref[:, E:] = feat_ref[:, pl.ds(start, E)]


def image_kernel(
    scale_ref, bias_ref, labels_ref, feat_ref, head_ref, txt_ref,
    unit_ref, inverse_ref, rows_ref, d_img_ref, d_txt_ref,
):
    proj = dot(feat_ref[...], head_ref[...])
    inverse = inverse_norm(proj)
    unit = proj * inverse
    rows = unit.astype(BF16)
    txt = txt_ref[...]
    unit_ref[...] = unit
    inverse_ref[...] = inverse
    rows_ref[...] = rows
    across = jnp.broadcast_to(labels_ref[...].astype(F32), (ROWS, ROWS))
    sign = jnp.where(across == across.T, 1.0, -1.0)
    logits = scale_ref[0] * dot(rows, txt, 1, 1) + bias_ref[0]
    grad = (-sign * jax.nn.sigmoid(-sign * logits)).astype(BF16)
    d_img_ref[...] = dot(grad, txt)
    d_txt_ref[...] = dot(grad, rows, 0, 0)


def pair_term(scale_ref, bias_ref, rows, others):
    logits = scale_ref[0] * dot(rows, others, 1, 1) + bias_ref[0]
    return dot(jax.nn.sigmoid(logits).astype(BF16), others)


def pair_kernel(scale_ref, bias_ref, total_ref, rows_ref, other_ref, out_ref):
    out_ref[...] = total_ref[...] + pair_term(scale_ref, bias_ref, rows_ref[...], other_ref[...])


def packed_text_kernel(scale_ref, bias_ref, total_ref, rows_ref, packed_ref, out_ref):
    term = pair_term(scale_ref, bias_ref, rows_ref[...], packed_ref[:, :E])
    out_ref[...] = total_ref[...] + term


def image_end_kernel(
    scale_ref, bias_ref, total_ref, rows_ref, other_ref, unit_ref, inverse_ref, packed_ref
):
    rows = rows_ref[...]
    total = total_ref[...] + pair_term(scale_ref, bias_ref, rows, other_ref[...])
    packed_ref[:, :E] = tangent(scale_ref[0] * total, unit_ref[...], inverse_ref[...])
    packed_ref[:, E:] = rows


def packed_image_kernel(scale_ref, bias_ref, total_ref, rows_ref, packed_ref, out_ref):
    out_ref[...] = total_ref[...] + pair_term(scale_ref, bias_ref, rows_ref[...], packed_ref[:, E:])


def text_end_kernel(scale_ref, bias_ref, total_ref, rows_ref, a_ref, b_ref, c_ref, txt_ref, out_ref):
    rows = rows_ref[...]
    total = total_ref[...]
    for other_ref in (a_ref, b_ref, c_ref):
        total = total + pair_term(scale_ref, bias_ref, rows, other_ref[...])
    value = txt_ref[...].astype(F32)
    inverse = inverse_norm(value)
    out_ref[...] = tangent(scale_ref[0] * total, value * inverse, inverse)


def head_kernel(core_ref, feat_ref, other_feat_ref, mine_ref, theirs_ref, out_ref):
    core = core_ref[0]
    mine, theirs = mine_ref[:, :E], theirs_ref[:, :E]

    def product(column):
        here = pl.multiple_of(column, 128)
        there = pl.multiple_of(E + column - 512 * core, 128)
        total = dot(feat_ref[:, pl.ds(here, 128)], mine, 0, 0)
        return total + dot(other_feat_ref[:, pl.ds(there, 128)], theirs, 0, 0)

    def store(band, rows):
        for t in range(5):
            slab = band * 5 + t
            out_ref[slab // SLABS, slab % SLABS] = rows[:, 128 * t : 128 * t + 128].astype(BF16)

    for block in range(4):
        total = product(5 * 128 * core + 128 * block)
        for j in range(8):
            store(8 * block + j, total[16 * j : 16 * j + 16])
    total = product(512)
    total = jnp.where(core == 0, total[:64], total[64:])
    for j in range(4):
        store(32 + j, total[16 * j : 16 * j + 16])
    out_ref[OWNERS - 1] = jnp.zeros((SLABS, 16, 128), BF16)


def place_kernel(core_ref, mine_ref, theirs_ref, out_ref, whole, sems):
    core = core_ref[0]
    copies = []
    for block in range(9):
        for band in range(8 * block, 8 * block + 8):
            owner = int(band >= 36)
            own = band if band < 36 else band - 40 if band >= 40 else band - 4
            for t in range(5):
                slab = own * 5 + t
                at = (slab // SLABS, slab % SLABS)
                value = jnp.where(core == owner, mine_ref[at], theirs_ref[at])
                whole[16 * band : 16 * band + 16, 128 * t : 128 * t + 128] = value
        rows = pl.ds(128 * block, 128)
        copies.append(pltpu.make_async_copy(whole.at[rows], out_ref.at[rows], sems.at[block]))
        copies[-1].start()
    for copy in copies:
        copy.wait()


def per_device(img_feat, head_weight, txt_emb, labels, log_logit_scale, bias):
    core = (lax.axis_index("dp") & 1)[None]
    scale = jnp.exp(log_logit_scale)
    pair = ROWS * ROWS * E * 4
    little = pair // 100
    block = shape(ROWS, E)
    block16 = shape(ROWS, E, dtype=BF16)

    pair16 = shape(ROWS, 2 * E, dtype=BF16)
    txt_rows, packed_txt = call(
        text_kernel, (block16, pair16), [SMEM, VMEM, VMEM], 1000000, core, txt_emb, img_feat
    )
    txt_15 = swap(txt_rows, 15)
    txt_7 = swap(txt_rows, 7)
    txt_3 = swap(txt_rows, 3)
    packed_txt = swap(packed_txt, 1)

    unit, inverse, img_rows, d_img, d_txt = call(
        image_kernel,
        (block, shape(ROWS, 1), block16, block, block),
        [SMEM, SMEM, VMEM, VMEM, VMEM, VMEM],
        12 * pair,
        scale, bias, labels[None, :], img_feat, head_weight, txt_rows,
    )
    pair_specs = [SMEM, SMEM, VMEM, VMEM, VMEM]
    for kernel, other in (
        (pair_kernel, txt_15), (pair_kernel, txt_3), (packed_text_kernel, packed_txt),
    ):
        d_img = call(kernel, block, pair_specs, little, scale, bias, d_img, img_rows, other)
    img_3 = swap(img_rows, 3)
    d_img = after(d_img, img_3)
    packed_img = call(
        image_end_kernel, pair16, pair_specs + [VMEM, VMEM], little,
        scale, bias, d_img, img_rows, txt_7, unit, inverse,
    )
    other_img = swap(packed_img, 1)

    parts = call(
        head_kernel, shape(OWNERS, SLABS, 16, 128, dtype=BF16), [SMEM] + [VMEM] * 4,
        4 * ROWS * D * E // 2, core, img_feat, packed_txt, packed_img, other_img,
    )
    total = jnp.sum(exchange(parts).astype(F32), axis=0)
    d_img_feat = dot(packed_img[:, :E], head_weight, 1, 1).astype(BF16)
    d_txt = call(
        packed_image_kernel, block, pair_specs, 2 * pair,
        scale, bias, d_txt, txt_rows, other_img,
    )
    images = [img_3]
    for z, beside, c in ((15, None, 7), (4, d_img_feat, 15), (2, d_txt, None), (1, None, None)):
        mine = total.astype(BF16)
        sent = mine if beside is None else after(mine, beside, *images)
        if c is not None:
            images.append(swap(after(img_rows, mine), c))
        total = mine.astype(F32) + swap(sent, z * 8).astype(F32)
    part = total.astype(BF16)
    parts = exchange(after(jnp.broadcast_to(part[None], (OWNERS, SLABS, 16, 128))))
    d_head = call(
        place_kernel, shape(D, E, dtype=BF16), [SMEM, VMEM, VMEM], 0,
        core, parts, swap(parts, 1),
        scratch=[pltpu.VMEM((D, E), BF16), pltpu.SemaphoreType.DMA((9,))],
        out_specs=pl.BlockSpec(memory_space=pl.ANY),
    )

    d_txt_emb = call(
        text_end_kernel, block16, pair_specs + [VMEM] * 3, 3 * pair,
        scale, bias, d_txt, txt_rows, *images, txt_emb,
    )
    return (d_img_feat, d_txt_emb, d_head)


def solution(mesh):
    return jax.shard_map(
        per_device,
        mesh=mesh,
        in_specs=(P("dp", None), P(), P("dp", None), P("dp"), P(), P()),
        out_specs=(P("dp", None), P("dp", None), P()),
        check_vma=False,
    )
```

```python
import jax
import jax.numpy as jnp
from jax import lax
from jax.experimental import pallas as pl
from jax.experimental.pallas import tpu as pltpu
from jax.sharding import PartitionSpec as P

D = 1152
E = 640
ROWS = 256
F32 = jnp.float32
BF16 = jnp.bfloat16
OWNERS, SLABS = 16, 12
SMEM = pl.BlockSpec(memory_space=pltpu.SMEM)
VMEM = pl.BlockSpec(memory_space=pltpu.VMEM)


def group(bits):
    mask = sum(1 << b for b in bits)
    members = [
        sum((k >> j & 1) << b for j, b in enumerate(bits)) for k in range(1 << len(bits))
    ]
    return [[base | m for m in members] for base in range(512) if not base & mask]


PLANE = group((1, 2, 7, 8))
LINE = group((3, 4, 5, 6))


def swap(value, mask):
    pairs = [(source, source ^ mask) for source in range(lax.axis_size("dp"))]
    return lax.ppermute(value, "dp", pairs)


def exchange(value, members):
    return lax.all_to_all(value, "dp", 0, 0, axis_index_groups=members, tiled=True)


def after(value, *others):
    return lax.optimization_barrier((value,) + others)[0]


def shape(*dims, dtype=F32):
    return jax.ShapeDtypeStruct(dims, dtype)


def dot(left, right, left_dim=1, right_dim=0):
    return lax.dot_general(
        left, right, (((left_dim,), (right_dim,)), ((), ())), preferred_element_type=F32
    )


def call(kernel, out_shape, specs, flops, *operands, scratch=(), out_specs=None):
    return pl.pallas_call(
        kernel,
        out_shape=out_shape,
        in_specs=specs,
        out_specs=out_specs if out_specs is not None else jax.tree.map(lambda _: VMEM, out_shape),
        scratch_shapes=scratch,
        compiler_params=pltpu.CompilerParams(vmem_limit_bytes=32 << 20),
        cost_estimate=pl.CostEstimate(flops=flops, bytes_accessed=100000, transcendentals=0),
    )(*operands)


def inverse_norm(value):
    return lax.rsqrt(jnp.sum(value * value, axis=-1, keepdims=True) + 1e-06)


def tangent(d_unit, unit, inverse):
    return ((d_unit - unit * jnp.sum(unit * d_unit, axis=-1, keepdims=True)) * inverse).astype(BF16)


def text_kernel(txt_ref, rows_ref):
    value = txt_ref[...].astype(F32)
    rows_ref[...] = (value * inverse_norm(value)).astype(BF16)


def image_kernel(
    core_ref, scale_ref, bias_ref, labels_ref, feat_ref, head_ref, txt_ref,
    unit_ref, inverse_ref, rows_ref, d_img_ref, d_txt_ref, other_ref,
):
    proj = dot(feat_ref[...], head_ref[...])
    inverse = inverse_norm(proj)
    unit = proj * inverse
    rows = unit.astype(BF16)
    txt = txt_ref[...]
    unit_ref[...] = unit
    inverse_ref[...] = inverse
    rows_ref[...] = rows
    across = jnp.broadcast_to(labels_ref[...].astype(F32), (ROWS, ROWS))
    sign = jnp.where(across == across.T, 1.0, -1.0)
    logits = scale_ref[0] * dot(rows, txt, 1, 1) + bias_ref[0]
    grad = (-sign * jax.nn.sigmoid(-sign * logits)).astype(BF16)
    d_img_ref[...] = dot(grad, txt)
    d_txt_ref[...] = dot(grad, rows, 0, 0)
    other_ref[...] = feat_ref[:, pl.ds(pl.multiple_of(512 * (1 - core_ref[0]), 128), E)]


def pair_term(scale_ref, bias_ref, rows, others):
    logits = scale_ref[0] * dot(rows, others, 1, 1) + bias_ref[0]
    return dot(jax.nn.sigmoid(logits).astype(BF16), others)


def pair_kernel(scale_ref, bias_ref, total_ref, rows_ref, other_ref, out_ref):
    out_ref[...] = total_ref[...] + pair_term(scale_ref, bias_ref, rows_ref[...], other_ref[...])


def image_end_kernel(
    scale_ref, bias_ref, total_ref, rows_ref, other_ref, unit_ref, inverse_ref, packed_ref
):
    rows = rows_ref[...]
    total = total_ref[...] + pair_term(scale_ref, bias_ref, rows, other_ref[...])
    packed_ref[:, :E] = tangent(scale_ref[0] * total, unit_ref[...], inverse_ref[...])
    packed_ref[:, E:] = rows


def text_end_kernel(
    scale_ref, bias_ref, total_ref, rows_ref, packed_ref, a_ref, b_ref, c_ref, txt_ref, out_ref
):
    rows = rows_ref[...]
    total = total_ref[...] + pair_term(scale_ref, bias_ref, rows, packed_ref[:, E:])
    for other_ref in (a_ref, b_ref, c_ref):
        total = total + pair_term(scale_ref, bias_ref, rows, other_ref[...])
    value = txt_ref[...].astype(F32)
    inverse = inverse_norm(value)
    out_ref[...] = tangent(scale_ref[0] * total, value * inverse, inverse)


def sum_of(parts_ref):
    total = parts_ref[0].astype(F32)
    for k in range(1, OWNERS):
        total = total + parts_ref[k].astype(F32)
    return total.astype(BF16)


def plane_sum_kernel(parts_ref, out_ref):
    out_ref[:SLABS] = sum_of(parts_ref)
    out_ref[SLABS:] = jnp.zeros((OWNERS - SLABS, 16, 128), BF16)


def line_sum_kernel(parts_ref, out_ref):
    out_ref[...] = jnp.broadcast_to(sum_of(parts_ref)[None], (OWNERS, 16, 128))


def head_kernel(core_ref, feat_ref, other_feat_ref, mine_ref, theirs_ref, out_ref):
    core = core_ref[0]
    mine, theirs = mine_ref[:, :E], theirs_ref[:, :E]

    def product(column):
        here = pl.multiple_of(column, 128)
        there = pl.multiple_of(column - 512 * core, 128)
        total = dot(feat_ref[:, pl.ds(here, 128)], mine, 0, 0)
        return total + dot(other_feat_ref[:, pl.ds(there, 128)], theirs, 0, 0)

    def store(band, rows):
        for t in range(5):
            slab = band * 5 + t
            out_ref[slab // SLABS, slab % SLABS] = rows[:, 128 * t : 128 * t + 128].astype(BF16)

    for block in range(4):
        total = product(5 * 128 * core + 128 * block)
        for j in range(8):
            store(8 * block + j, total[16 * j : 16 * j + 16])
    total = product(512)
    total = jnp.where(core == 0, total[:64], total[64:])
    for j in range(4):
        store(32 + j, total[16 * j : 16 * j + 16])
    out_ref[OWNERS - 1] = jnp.zeros((SLABS, 16, 128), BF16)


def place_kernel(core_ref, mine_ref, theirs_ref, out_ref, whole, sems):
    core = core_ref[0]
    copies = []
    for block in range(9):
        for band in range(8 * block, 8 * block + 8):
            owner = int(band >= 36)
            own = band if band < 36 else band - 40 if band >= 40 else band - 4
            for t in range(5):
                slab = own * 5 + t
                at = (slab // SLABS, slab % SLABS)
                value = jnp.where(core == owner, mine_ref[at], theirs_ref[at])
                whole[16 * band : 16 * band + 16, 128 * t : 128 * t + 128] = value
        rows = pl.ds(128 * block, 128)
        copies.append(pltpu.make_async_copy(whole.at[rows], out_ref.at[rows], sems.at[block]))
        copies[-1].start()
    for copy in copies:
        copy.wait()


def per_device(img_feat, head_weight, txt_emb, labels, log_logit_scale, bias):
    core = (lax.axis_index("dp") & 1)[None]
    scale = jnp.exp(log_logit_scale)
    pair = ROWS * ROWS * E * 4
    little = pair // 100
    block = shape(ROWS, E)
    block16 = shape(ROWS, E, dtype=BF16)

    pair16 = shape(ROWS, 2 * E, dtype=BF16)
    txt_rows = call(text_kernel, block16, [VMEM], 1000000, txt_emb)
    text = {c: swap(txt_rows, c) for c in (15, 3, 1, 7)}

    unit, inverse, img_rows, d_img, d_txt, other_feat = call(
        image_kernel,
        (block, shape(ROWS, 1), block16, block, block, block16),
        [SMEM, SMEM, SMEM, VMEM, VMEM, VMEM, VMEM],
        12 * pair,
        core, scale, bias, labels[None, :], img_feat, head_weight, txt_rows,
    )
    other_feat = swap(other_feat, 1)
    pair_specs = [SMEM, SMEM, VMEM, VMEM, VMEM]
    for c in (15, 3, 1):
        d_img = call(pair_kernel, block, pair_specs, little, scale, bias, d_img, img_rows, text[c])
    packed_img = call(
        image_end_kernel, pair16, pair_specs + [VMEM, VMEM], little,
        scale, bias, d_img, img_rows, text[7], unit, inverse,
    )
    other_img = swap(after(packed_img, other_feat), 1)
    d_img_feat = dot(packed_img[:, :E], head_weight, 1, 1).astype(BF16)

    parts = call(
        head_kernel, shape(OWNERS, SLABS, 16, 128, dtype=BF16), [SMEM] + [VMEM] * 4,
        4 * ROWS * D * E // 2, core, img_feat, other_feat, packed_img, other_img,
    )
    parts = exchange(after(parts, d_img_feat), PLANE)
    line = shape(OWNERS, 16, 128, dtype=BF16)
    part = call(plane_sum_kernel, line, [VMEM], little, parts)
    late = after(img_rows, part)
    images = [swap(late, c) for c in (7, 15, 3)]
    part = call(line_sum_kernel, line, [VMEM], little, exchange(part, LINE))
    part = exchange(part, LINE)[:SLABS]
    part = after(part, *images)
    parts = exchange(after(jnp.broadcast_to(part[None], (OWNERS, SLABS, 16, 128))), PLANE)
    d_head = call(
        place_kernel, shape(D, E, dtype=BF16), [SMEM, VMEM, VMEM], 0,
        core, parts, swap(parts, 1),
        scratch=[pltpu.VMEM((D, E), BF16), pltpu.SemaphoreType.DMA((9,))],
        out_specs=pl.BlockSpec(memory_space=pl.ANY),
    )

    d_txt_emb = call(
        text_end_kernel, block16, pair_specs + [VMEM] * 4, 4 * pair,
        scale, bias, d_txt, txt_rows, other_img, *images, txt_emb,
    )
    return (d_img_feat, d_txt_emb, d_head)


def solution(mesh):
    return jax.shard_map(
        per_device,
        mesh=mesh,
        in_specs=(P("dp", None), P(), P("dp", None), P("dp"), P(), P()),
        out_specs=(P("dp", None), P("dp", None), P()),
        check_vma=False,
    )
```

```python
import jax
import jax.numpy as jnp
from jax import lax
from jax.experimental import pallas as pl
from jax.experimental.pallas import tpu as pltpu
from jax.sharding import PartitionSpec as P

D = 1152
E = 640
ROWS = 256
F32 = jnp.float32
BF16 = jnp.bfloat16
OWNERS, SLABS = 16, 12
SMEM = pl.BlockSpec(memory_space=pltpu.SMEM)
VMEM = pl.BlockSpec(memory_space=pltpu.VMEM)


def group(bits):
    mask = sum(1 << b for b in bits)
    members = [
        sum((k >> j & 1) << b for j, b in enumerate(bits)) for k in range(1 << len(bits))
    ]
    return [[base | m for m in members] for base in range(512) if not base & mask]


PLANE = group((1, 2, 7, 8))
NEAR, FAR = group((3, 4)), group((5, 6))


def swap(value, mask):
    pairs = [(source, source ^ mask) for source in range(lax.axis_size("dp"))]
    return lax.ppermute(value, "dp", pairs)


def exchange(value, members):
    return lax.all_to_all(value, "dp", 0, 0, axis_index_groups=members, tiled=True)


def after(value, *others):
    return lax.optimization_barrier((value,) + others)[0]


def shape(*dims, dtype=F32):
    return jax.ShapeDtypeStruct(dims, dtype)


def dot(left, right, left_dim=1, right_dim=0):
    return lax.dot_general(
        left, right, (((left_dim,), (right_dim,)), ((), ())), preferred_element_type=F32
    )


def call(kernel, out_shape, specs, flops, *operands, scratch=(), out_specs=None):
    return pl.pallas_call(
        kernel,
        out_shape=out_shape,
        in_specs=specs,
        out_specs=out_specs if out_specs is not None else jax.tree.map(lambda _: VMEM, out_shape),
        scratch_shapes=scratch,
        compiler_params=pltpu.CompilerParams(vmem_limit_bytes=32 << 20),
        cost_estimate=pl.CostEstimate(flops=flops, bytes_accessed=100000, transcendentals=0),
    )(*operands)


def inverse_norm(value):
    return lax.rsqrt(jnp.sum(value * value, axis=-1, keepdims=True) + 1e-06)


def tangent(d_unit, unit, inverse):
    return ((d_unit - unit * jnp.sum(unit * d_unit, axis=-1, keepdims=True)) * inverse).astype(BF16)


def text_kernel(txt_ref, rows_ref):
    value = txt_ref[...].astype(F32)
    rows_ref[...] = (value * inverse_norm(value)).astype(BF16)


def image_kernel(
    core_ref, scale_ref, bias_ref, labels_ref, feat_ref, head_ref, txt_ref,
    unit_ref, inverse_ref, rows_ref, d_img_ref, d_txt_ref, other_ref,
):
    proj = dot(feat_ref[...], head_ref[...])
    inverse = inverse_norm(proj)
    unit = proj * inverse
    rows = unit.astype(BF16)
    txt = txt_ref[...]
    unit_ref[...] = unit
    inverse_ref[...] = inverse
    rows_ref[...] = rows
    across = jnp.broadcast_to(labels_ref[...].astype(F32), (ROWS, ROWS))
    sign = jnp.where(across == across.T, 1.0, -1.0)
    logits = scale_ref[0] * dot(rows, txt, 1, 1) + bias_ref[0]
    grad = (-sign * jax.nn.sigmoid(-sign * logits)).astype(BF16)
    d_img_ref[...] = dot(grad, txt)
    d_txt_ref[...] = dot(grad, rows, 0, 0)
    other_ref[...] = feat_ref[:, pl.ds(pl.multiple_of(512 * (1 - core_ref[0]), 128), E)]


def pair_term(scale_ref, bias_ref, rows, others):
    logits = scale_ref[0] * dot(rows, others, 1, 1) + bias_ref[0]
    return dot(jax.nn.sigmoid(logits).astype(BF16), others)


def pair_kernel(scale_ref, bias_ref, total_ref, rows_ref, other_ref, out_ref):
    out_ref[...] = total_ref[...] + pair_term(scale_ref, bias_ref, rows_ref[...], other_ref[...])


def image_end_kernel(
    scale_ref, bias_ref, total_ref, rows_ref, other_ref, unit_ref, inverse_ref, feat_ref, packed_ref
):
    rows = rows_ref[...]
    total = total_ref[...] + pair_term(scale_ref, bias_ref, rows, other_ref[...])
    packed_ref[:, :E] = tangent(scale_ref[0] * total, unit_ref[...], inverse_ref[...])
    packed_ref[:, E : 2 * E] = rows
    packed_ref[:, 2 * E :] = feat_ref[...]


def text_end_kernel(
    scale_ref, bias_ref, total_ref, rows_ref, packed_ref, a_ref, b_ref, c_ref, txt_ref, out_ref
):
    rows = rows_ref[...]
    total = total_ref[...] + pair_term(scale_ref, bias_ref, rows, packed_ref[:, E : 2 * E])
    for other_ref in (a_ref, b_ref, c_ref):
        total = total + pair_term(scale_ref, bias_ref, rows, other_ref[...])
    value = txt_ref[...].astype(F32)
    inverse = inverse_norm(value)
    out_ref[...] = tangent(scale_ref[0] * total, value * inverse, inverse)


def sum_kernel(parts_ref, out_ref):
    total = parts_ref[0].astype(F32)
    for k in range(1, parts_ref.shape[0]):
        total = total + parts_ref[k].astype(F32)
    out_ref[...] = total.astype(BF16)


def spread_sum_kernel(parts_ref, out_ref):
    total = parts_ref[0].astype(F32)
    for k in range(1, parts_ref.shape[0]):
        total = total + parts_ref[k].astype(F32)
    out_ref[...] = jnp.broadcast_to(total.astype(BF16)[None], out_ref.shape)


def head_kernel(core_ref, feat_ref, mine_ref, theirs_ref, out_ref):
    core = core_ref[0]
    mine, theirs = mine_ref[:, :E], theirs_ref[:, :E]

    def product(column):
        here = pl.multiple_of(column, 128)
        there = pl.multiple_of(2 * E + column - 512 * core, 128)
        total = dot(feat_ref[:, pl.ds(here, 128)], mine, 0, 0)
        return total + dot(theirs_ref[:, pl.ds(there, 128)], theirs, 0, 0)

    def store(band, rows):
        for t in range(5):
            slab = band * 5 + t
            out_ref[slab // SLABS, slab % SLABS] = rows[:, 128 * t : 128 * t + 128].astype(BF16)

    for block in range(4):
        total = product(5 * 128 * core + 128 * block)
        for j in range(8):
            store(8 * block + j, total[16 * j : 16 * j + 16])
    total = product(512)
    total = jnp.where(core == 0, total[:64], total[64:])
    for j in range(4):
        store(32 + j, total[16 * j : 16 * j + 16])
    out_ref[OWNERS - 1] = jnp.zeros((SLABS, 16, 128), BF16)


def place_kernel(core_ref, mine_ref, theirs_ref, out_ref, whole, sems):
    core = core_ref[0]
    copies = []
    for block in range(9):
        for band in range(8 * block, 8 * block + 8):
            owner = int(band >= 36)
            own = band if band < 36 else band - 40 if band >= 40 else band - 4
            for t in range(5):
                slab = own * 5 + t
                at = (slab // SLABS, slab % SLABS)
                value = jnp.where(core == owner, mine_ref[at], theirs_ref[at])
                whole[16 * band : 16 * band + 16, 128 * t : 128 * t + 128] = value
        rows = pl.ds(128 * block, 128)
        copies.append(pltpu.make_async_copy(whole.at[rows], out_ref.at[rows], sems.at[block]))
        copies[-1].start()
    for copy in copies:
        copy.wait()


def per_device(img_feat, head_weight, txt_emb, labels, log_logit_scale, bias):
    core = (lax.axis_index("dp") & 1)[None]
    scale = jnp.exp(log_logit_scale)
    pair = ROWS * ROWS * E * 4
    little = pair // 100
    block = shape(ROWS, E)
    block16 = shape(ROWS, E, dtype=BF16)

    packed = shape(ROWS, 3 * E, dtype=BF16)
    txt_rows = call(text_kernel, block16, [VMEM], 40 * pair, txt_emb)
    text = {c: swap(txt_rows, c) for c in (15, 3, 1, 7)}

    unit, inverse, img_rows, d_img, d_txt, other_feat = call(
        image_kernel,
        (block, shape(ROWS, 1), block16, block, block, block16),
        [SMEM, SMEM, SMEM, VMEM, VMEM, VMEM, VMEM],
        12 * pair,
        core, scale, bias, labels[None, :], img_feat, head_weight, txt_rows,
    )
    img_3 = swap(img_rows, 3)
    pair_specs = [SMEM, SMEM, VMEM, VMEM, VMEM]
    for c in (15, 3, 1):
        d_img = call(pair_kernel, block, pair_specs, little, scale, bias, d_img, img_rows, text[c])
    packed_img = call(
        image_end_kernel, packed, pair_specs + [VMEM] * 3, little,
        scale, bias, d_img, img_rows, text[7], unit, inverse, other_feat,
    )
    other_img = swap(after(packed_img, img_3), 1)
    d_img_feat = dot(packed_img[:, :E], head_weight, 1, 1).astype(BF16)

    parts = call(
        head_kernel, shape(OWNERS, SLABS, 16, 128, dtype=BF16), [SMEM] + [VMEM] * 3,
        4 * ROWS * D * E // 2, core, img_feat, packed_img, other_img,
    )
    parts = exchange(after(parts, d_img_feat), PLANE)
    slab = (16, 128)
    part = call(sum_kernel, shape(SLABS, *slab, dtype=BF16), [VMEM], little, parts)
    late = after(img_rows, part)
    images = [img_3, swap(late, 7), swap(late, 15)]
    quarters = shape(4, SLABS // 4, *slab, dtype=BF16)
    parts = exchange(part.reshape(quarters.shape), NEAR)
    parts = exchange(call(spread_sum_kernel, quarters, [VMEM], little, parts), FAR)
    parts = exchange(call(spread_sum_kernel, quarters, [VMEM], little, parts), NEAR)
    part = after(parts.reshape(SLABS, *slab), *images)
    parts = exchange(after(jnp.broadcast_to(part[None], (OWNERS, SLABS, 16, 128))), PLANE)
    d_head = call(
        place_kernel, shape(D, E, dtype=BF16), [SMEM, VMEM, VMEM], 0,
        core, parts, swap(parts, 1),
        scratch=[pltpu.VMEM((D, E), BF16), pltpu.SemaphoreType.DMA((9,))],
        out_specs=pl.BlockSpec(memory_space=pl.ANY),
    )

    d_txt_emb = call(
        text_end_kernel, block16, pair_specs + [VMEM] * 4, 4 * pair,
        scale, bias, d_txt, txt_rows, other_img, *images, txt_emb,
    )
    return (d_img_feat, d_txt_emb, d_head)


def solution(mesh):
    return jax.shard_map(
        per_device,
        mesh=mesh,
        in_specs=(P("dp", None), P(), P("dp", None), P("dp"), P(), P()),
        out_specs=(P("dp", None), P("dp", None), P()),
        check_vma=False,
    )
```

```python
import jax
import jax.numpy as jnp
from jax import lax
from jax.experimental import pallas as pl
from jax.experimental.pallas import tpu as pltpu
from jax.sharding import PartitionSpec as P

D = 1152
E = 640
ROWS = 256
F32 = jnp.float32
BF16 = jnp.bfloat16
OWNERS, SLABS = 16, 12
SMEM = pl.BlockSpec(memory_space=pltpu.SMEM)
VMEM = pl.BlockSpec(memory_space=pltpu.VMEM)


def group(bits):
    mask = sum(1 << b for b in bits)
    members = [
        sum((k >> j & 1) << b for j, b in enumerate(bits)) for k in range(1 << len(bits))
    ]
    return [[base | m for m in members] for base in range(512) if not base & mask]


PLANE = group((1, 2, 7, 8))
NEAR, FAR = group((3, 4)), group((5, 6))


def swap(value, mask):
    pairs = [(source, source ^ mask) for source in range(lax.axis_size("dp"))]
    return lax.ppermute(value, "dp", pairs)


def exchange(value, members):
    return lax.all_to_all(value, "dp", 0, 0, axis_index_groups=members, tiled=True)


def after(value, *others):
    return lax.optimization_barrier((value,) + others)[0]


def shape(*dims, dtype=F32):
    return jax.ShapeDtypeStruct(dims, dtype)


def dot(left, right, left_dim=1, right_dim=0):
    return lax.dot_general(
        left, right, (((left_dim,), (right_dim,)), ((), ())), preferred_element_type=F32
    )


def call(kernel, out_shape, specs, flops, *operands, scratch=(), out_specs=None):
    return pl.pallas_call(
        kernel,
        out_shape=out_shape,
        in_specs=specs,
        out_specs=out_specs if out_specs is not None else jax.tree.map(lambda _: VMEM, out_shape),
        scratch_shapes=scratch,
        compiler_params=pltpu.CompilerParams(vmem_limit_bytes=14 << 20),
        cost_estimate=pl.CostEstimate(flops=flops, bytes_accessed=100000, transcendentals=0),
    )(*operands)


def inverse_norm(value):
    return lax.rsqrt(jnp.sum(value * value, axis=-1, keepdims=True) + 1e-06)


def tangent(d_unit, unit, inverse):
    return ((d_unit - unit * jnp.sum(unit * d_unit, axis=-1, keepdims=True)) * inverse).astype(BF16)


def text_kernel(txt_ref, rows_ref):
    value = txt_ref[...].astype(F32)
    rows_ref[...] = (value * inverse_norm(value)).astype(BF16)


def image_kernel(
    core_ref, scale_ref, bias_ref, labels_ref, feat_ref, head_ref, txt_ref,
    unit_ref, inverse_ref, rows_ref, d_img_ref, d_txt_ref, other_ref,
):
    proj = dot(feat_ref[...], head_ref[...])
    inverse = inverse_norm(proj)
    unit = proj * inverse
    rows = unit.astype(BF16)
    txt = txt_ref[...]
    unit_ref[...] = unit
    inverse_ref[...] = inverse
    rows_ref[...] = rows
    across = jnp.broadcast_to(labels_ref[...].astype(F32), (ROWS, ROWS))
    sign = jnp.where(across == across.T, 1.0, -1.0)
    logits = scale_ref[0] * dot(rows, txt, 1, 1) + bias_ref[0]
    grad = (-sign * jax.nn.sigmoid(-sign * logits)).astype(BF16)
    d_img_ref[...] = dot(grad, txt)
    d_txt_ref[...] = dot(grad, rows, 0, 0)
    other_ref[...] = feat_ref[:, pl.ds(pl.multiple_of(512 * (1 - core_ref[0]), 128), E)]


def pair_term(scale_ref, bias_ref, rows, others):
    logits = scale_ref[0] * dot(rows, others, 1, 1) + bias_ref[0]
    return dot(jax.nn.sigmoid(logits).astype(BF16), others)


def pair_kernel(scale_ref, bias_ref, total_ref, rows_ref, other_ref, out_ref):
    out_ref[...] = total_ref[...] + pair_term(scale_ref, bias_ref, rows_ref[...], other_ref[...])


def image_end_kernel(
    scale_ref, bias_ref, total_ref, rows_ref, other_ref, unit_ref, inverse_ref, feat_ref, packed_ref
):
    rows = rows_ref[...]
    total = total_ref[...] + pair_term(scale_ref, bias_ref, rows, other_ref[...])
    packed_ref[:, :E] = tangent(scale_ref[0] * total, unit_ref[...], inverse_ref[...])
    packed_ref[:, E : 2 * E] = rows
    packed_ref[:, 2 * E :] = feat_ref[...]


def text_end_kernel(
    scale_ref, bias_ref, total_ref, rows_ref, packed_ref, a_ref, b_ref, c_ref, txt_ref, out_ref
):
    rows = rows_ref[...]
    total = total_ref[...] + pair_term(scale_ref, bias_ref, rows, packed_ref[:, E : 2 * E])
    for other_ref in (a_ref, b_ref, c_ref):
        total = total + pair_term(scale_ref, bias_ref, rows, other_ref[...])
    value = txt_ref[...].astype(F32)
    inverse = inverse_norm(value)
    out_ref[...] = tangent(scale_ref[0] * total, value * inverse, inverse)


def sum_kernel(parts_ref, out_ref):
    total = parts_ref[0].astype(F32)
    for k in range(1, parts_ref.shape[0]):
        total = total + parts_ref[k].astype(F32)
    out_ref[...] = total.astype(BF16)


def spread_sum_kernel(parts_ref, out_ref):
    total = parts_ref[0].astype(F32)
    for k in range(1, parts_ref.shape[0]):
        total = total + parts_ref[k].astype(F32)
    out_ref[...] = jnp.broadcast_to(total.astype(BF16)[None], out_ref.shape)


def head_kernel(core_ref, feat_ref, mine_ref, theirs_ref, out_ref):
    core = core_ref[0]
    mine, theirs = mine_ref[:, :E], theirs_ref[:, :E]

    def product(column):
        here = pl.multiple_of(column, 128)
        there = pl.multiple_of(2 * E + column - 512 * core, 128)
        total = dot(feat_ref[:, pl.ds(here, 128)], mine, 0, 0)
        return total + dot(theirs_ref[:, pl.ds(there, 128)], theirs, 0, 0)

    def store(band, rows):
        for t in range(5):
            slab = band * 5 + t
            out_ref[slab // SLABS, slab % SLABS] = rows[:, 128 * t : 128 * t + 128].astype(BF16)

    for block in range(4):
        total = product(5 * 128 * core + 128 * block)
        for j in range(8):
            store(8 * block + j, total[16 * j : 16 * j + 16])
    total = product(512)
    total = jnp.where(core == 0, total[:64], total[64:])
    for j in range(4):
        store(32 + j, total[16 * j : 16 * j + 16])
    out_ref[OWNERS - 1] = jnp.zeros((SLABS, 16, 128), BF16)


def place_kernel(core_ref, mine_ref, theirs_ref, out_ref, whole, sems):
    core = core_ref[0]
    copies = []
    for block in range(9):
        for band in range(8 * block, 8 * block + 8):
            owner = int(band >= 36)
            own = band if band < 36 else band - 40 if band >= 40 else band - 4
            for t in range(5):
                slab = own * 5 + t
                at = (slab // SLABS, slab % SLABS)
                value = jnp.where(core == owner, mine_ref[at], theirs_ref[at])
                whole[16 * band : 16 * band + 16, 128 * t : 128 * t + 128] = value
        rows = pl.ds(128 * block, 128)
        copies.append(pltpu.make_async_copy(whole.at[rows], out_ref.at[rows], sems.at[block]))
        copies[-1].start()
    for copy in copies:
        copy.wait()


def per_device(img_feat, head_weight, txt_emb, labels, log_logit_scale, bias):
    core = (lax.axis_index("dp") & 1)[None]
    scale = jnp.exp(log_logit_scale)
    pair = ROWS * ROWS * E * 4
    little = pair // 100
    block = shape(ROWS, E)
    block16 = shape(ROWS, E, dtype=BF16)

    packed = shape(ROWS, 3 * E, dtype=BF16)
    txt_rows = call(text_kernel, block16, [VMEM], 40 * pair, txt_emb)
    txt_7 = swap(txt_rows, 7)
    unit, inverse, img_rows, d_img, d_txt, other_feat = call(
        image_kernel,
        (block, shape(ROWS, 1), block16, block, block, block16),
        [SMEM, SMEM, SMEM, VMEM, VMEM, VMEM, VMEM],
        12 * pair,
        core, scale, bias, labels[None, :], img_feat, head_weight, txt_rows,
    )
    late = after(txt_rows, img_rows)
    txt_3, txt_1 = swap(late, 3), swap(late, 1)
    img_7, img_3 = swap(img_rows, 7), swap(img_rows, 3)
    txt_15, img_15 = swap(txt_7, 8), swap(img_7, 8)
    pair_specs = [SMEM, SMEM, VMEM, VMEM, VMEM]
    for other in (txt_7, txt_3, txt_1):
        d_img = call(pair_kernel, block, pair_specs, little, scale, bias, d_img, img_rows, other)
    packed_img = call(
        image_end_kernel, packed, pair_specs + [VMEM] * 3, little,
        scale, bias, d_img, img_rows, txt_15, unit, inverse, other_feat,
    )
    other_img = swap(after(packed_img, img_3, img_7), 1)
    d_img_feat = dot(packed_img[:, :E], head_weight, 1, 1).astype(BF16)

    parts = call(
        head_kernel, shape(OWNERS, SLABS, 16, 128, dtype=BF16), [SMEM] + [VMEM] * 3,
        4 * ROWS * D * E // 2, core, img_feat, packed_img, other_img,
    )
    parts = exchange(after(parts, d_img_feat), PLANE)
    slab = (16, 128)
    part = call(sum_kernel, shape(SLABS, *slab, dtype=BF16), [VMEM], little, parts)
    part = after(part, img_15)
    quarters = shape(4, SLABS // 4, *slab, dtype=BF16)
    parts = exchange(part.reshape(quarters.shape), NEAR)
    parts = exchange(call(spread_sum_kernel, quarters, [VMEM], little, parts), FAR)
    parts = exchange(call(spread_sum_kernel, quarters, [VMEM], little, parts), NEAR)
    part = parts.reshape(SLABS, *slab)
    parts = exchange(after(jnp.broadcast_to(part[None], (OWNERS, SLABS, 16, 128))), PLANE)
    d_head = call(
        place_kernel, shape(D, E, dtype=BF16), [SMEM, VMEM, VMEM], 0,
        core, parts, swap(parts, 1),
        scratch=[pltpu.VMEM((D, E), BF16), pltpu.SemaphoreType.DMA((9,))],
        out_specs=pl.BlockSpec(memory_space=pl.ANY),
    )

    d_txt_emb = call(
        text_end_kernel, block16, pair_specs + [VMEM] * 4, 4 * pair,
        scale, bias, d_txt, txt_rows, other_img, img_3, img_7, img_15, txt_emb,
    )
    return (d_img_feat, d_txt_emb, d_head)


def solution(mesh):
    return jax.shard_map(
        per_device,
        mesh=mesh,
        in_specs=(P("dp", None), P(), P("dp", None), P("dp"), P(), P()),
        out_specs=(P("dp", None), P("dp", None), P()),
        check_vma=False,
    )
```

```python
import jax
import jax.numpy as jnp
from jax import lax
from jax.experimental import pallas as pl
from jax.experimental.pallas import tpu as pltpu
from jax.sharding import PartitionSpec as P

D = 1152
E = 640
ROWS = 256
F32 = jnp.float32
BF16 = jnp.bfloat16
OWNERS, SLABS = 16, 12
SMEM = pl.BlockSpec(memory_space=pltpu.SMEM)
VMEM = pl.BlockSpec(memory_space=pltpu.VMEM)


def group(bits):
    mask = sum(1 << b for b in bits)
    members = [
        sum((k >> j & 1) << b for j, b in enumerate(bits)) for k in range(1 << len(bits))
    ]
    return [[base | m for m in members] for base in range(512) if not base & mask]


PLANE = group((1, 2, 7, 8))
NEAR, FAR = group((3, 4)), group((5, 6))


def swap(value, mask):
    pairs = [(source, source ^ mask) for source in range(lax.axis_size("dp"))]
    return lax.ppermute(value, "dp", pairs)


def exchange(value, members):
    return lax.all_to_all(value, "dp", 0, 0, axis_index_groups=members, tiled=True)


def after(value, *others):
    return lax.optimization_barrier((value,) + others)[0]


def shape(*dims, dtype=F32):
    return jax.ShapeDtypeStruct(dims, dtype)


def dot(left, right, left_dim=1, right_dim=0):
    return lax.dot_general(
        left, right, (((left_dim,), (right_dim,)), ((), ())), preferred_element_type=F32
    )


def call(kernel, out_shape, specs, flops, *operands, scratch=(), out_specs=None):
    return pl.pallas_call(
        kernel,
        out_shape=out_shape,
        in_specs=specs,
        out_specs=out_specs if out_specs is not None else jax.tree.map(lambda _: VMEM, out_shape),
        scratch_shapes=scratch,
        compiler_params=pltpu.CompilerParams(vmem_limit_bytes=14 << 20),
        cost_estimate=pl.CostEstimate(flops=flops, bytes_accessed=100000, transcendentals=0),
    )(*operands)


def inverse_norm(value):
    return lax.rsqrt(jnp.sum(value * value, axis=-1, keepdims=True) + 1e-06)


def tangent(d_unit, unit, inverse):
    return ((d_unit - unit * jnp.sum(unit * d_unit, axis=-1, keepdims=True)) * inverse).astype(BF16)


def text_kernel(txt_ref, rows_ref):
    value = txt_ref[...].astype(F32)
    rows_ref[...] = (value * inverse_norm(value)).astype(BF16)


def image_kernel(
    core_ref, scale_ref, bias_ref, labels_ref, feat_ref, head_ref, txt_ref,
    unit_ref, inverse_ref, rows_ref, d_img_ref, d_txt_ref, other_ref,
):
    proj = dot(feat_ref[...], head_ref[...])
    inverse = inverse_norm(proj)
    unit = proj * inverse
    rows = unit.astype(BF16)
    txt = txt_ref[...]
    unit_ref[...] = unit
    inverse_ref[...] = inverse
    rows_ref[...] = rows
    across = jnp.broadcast_to(labels_ref[...].astype(F32), (ROWS, ROWS))
    sign = jnp.where(across == across.T, 1.0, -1.0)
    logits = scale_ref[0] * dot(rows, txt, 1, 1) + bias_ref[0]
    grad = (-sign * jax.nn.sigmoid(-sign * logits)).astype(BF16)
    d_img_ref[...] = dot(grad, txt)
    d_txt_ref[...] = dot(grad, rows, 0, 0)
    other_ref[...] = feat_ref[:, pl.ds(pl.multiple_of(512 * (1 - core_ref[0]), 128), E)]


def pair_term(scale_ref, bias_ref, rows, others):
    logits = scale_ref[0] * dot(rows, others, 1, 1) + bias_ref[0]
    return dot(jax.nn.sigmoid(logits).astype(BF16), others)


def pair_kernel(scale_ref, bias_ref, total_ref, rows_ref, other_ref, out_ref):
    out_ref[...] = total_ref[...] + pair_term(scale_ref, bias_ref, rows_ref[...], other_ref[...])


def image_end_kernel(
    scale_ref, bias_ref, total_ref, rows_ref, other_ref, unit_ref, inverse_ref, feat_ref, packed_ref
):
    rows = rows_ref[...]
    total = total_ref[...] + pair_term(scale_ref, bias_ref, rows, other_ref[...])
    packed_ref[:, :E] = tangent(scale_ref[0] * total, unit_ref[...], inverse_ref[...])
    packed_ref[:, E : 2 * E] = rows
    packed_ref[:, 2 * E :] = feat_ref[...]


def text_pairs_kernel(scale_ref, bias_ref, total_ref, rows_ref, packed_ref, other_ref, out_ref):
    rows = rows_ref[...]
    total = total_ref[...] + pair_term(scale_ref, bias_ref, rows, packed_ref[:, E : 2 * E])
    out_ref[...] = total + pair_term(scale_ref, bias_ref, rows, other_ref[...])


def text_end_kernel(scale_ref, bias_ref, total_ref, rows_ref, a_ref, b_ref, txt_ref, out_ref):
    rows = rows_ref[...]
    total = total_ref[...]
    for other_ref in (a_ref, b_ref):
        total = total + pair_term(scale_ref, bias_ref, rows, other_ref[...])
    value = txt_ref[...].astype(F32)
    inverse = inverse_norm(value)
    out_ref[...] = tangent(scale_ref[0] * total, value * inverse, inverse)


def sum_kernel(parts_ref, out_ref):
    total = parts_ref[0].astype(F32)
    for k in range(1, parts_ref.shape[0]):
        total = total + parts_ref[k].astype(F32)
    out_ref[...] = total.astype(BF16)


def spread_sum_kernel(parts_ref, out_ref):
    total = parts_ref[0].astype(F32)
    for k in range(1, parts_ref.shape[0]):
        total = total + parts_ref[k].astype(F32)
    out_ref[...] = jnp.broadcast_to(total.astype(BF16)[None], out_ref.shape)


def head_kernel(core_ref, feat_ref, mine_ref, theirs_ref, out_ref):
    core = core_ref[0]
    mine, theirs = mine_ref[:, :E], theirs_ref[:, :E]

    def product(column):
        here = pl.multiple_of(column, 128)
        there = pl.multiple_of(2 * E + column - 512 * core, 128)
        total = dot(feat_ref[:, pl.ds(here, 128)], mine, 0, 0)
        return total + dot(theirs_ref[:, pl.ds(there, 128)], theirs, 0, 0)

    def store(band, rows):
        for t in range(5):
            slab = band * 5 + t
            out_ref[slab // SLABS, slab % SLABS] = rows[:, 128 * t : 128 * t + 128].astype(BF16)

    for block in range(4):
        total = product(5 * 128 * core + 128 * block)
        for j in range(8):
            store(8 * block + j, total[16 * j : 16 * j + 16])
    total = product(512)
    total = jnp.where(core == 0, total[:64], total[64:])
    for j in range(4):
        store(32 + j, total[16 * j : 16 * j + 16])
    out_ref[OWNERS - 1] = jnp.zeros((SLABS, 16, 128), BF16)


def place_kernel(core_ref, mine_ref, theirs_ref, out_ref, whole, sems):
    core = core_ref[0]
    copies = []
    for block in range(9):
        for band in range(8 * block, 8 * block + 8):
            owner = int(band >= 36)
            own = band if band < 36 else band - 40 if band >= 40 else band - 4
            for t in range(5):
                slab = own * 5 + t
                at = (slab // SLABS, slab % SLABS)
                value = jnp.where(core == owner, mine_ref[at], theirs_ref[at])
                whole[16 * band : 16 * band + 16, 128 * t : 128 * t + 128] = value
        rows = pl.ds(128 * block, 128)
        copies.append(pltpu.make_async_copy(whole.at[rows], out_ref.at[rows], sems.at[block]))
        copies[-1].start()
    for copy in copies:
        copy.wait()


def per_device(img_feat, head_weight, txt_emb, labels, log_logit_scale, bias):
    core = (lax.axis_index("dp") & 1)[None]
    scale = jnp.exp(log_logit_scale)
    pair = ROWS * ROWS * E * 4
    little = pair // 100
    block = shape(ROWS, E)
    block16 = shape(ROWS, E, dtype=BF16)

    packed = shape(ROWS, 3 * E, dtype=BF16)
    txt_rows = call(text_kernel, block16, [VMEM], 40 * pair, txt_emb)
    txt_7 = swap(txt_rows, 7)
    unit, inverse, img_rows, d_img, d_txt, other_feat = call(
        image_kernel,
        (block, shape(ROWS, 1), block16, block, block, block16),
        [SMEM, SMEM, SMEM, VMEM, VMEM, VMEM, VMEM],
        12 * pair,
        core, scale, bias, labels[None, :], img_feat, head_weight, txt_rows,
    )
    late = after(txt_rows, img_rows)
    txt_3, txt_1 = swap(late, 3), swap(late, 1)
    img_7, img_3 = swap(img_rows, 7), swap(img_rows, 3)
    txt_15 = swap(txt_7, 8)
    pair_specs = [SMEM, SMEM, VMEM, VMEM, VMEM]
    for other in (txt_7, txt_3, txt_1):
        d_img = call(pair_kernel, block, pair_specs, little, scale, bias, d_img, img_rows, other)
    d_img = after(d_img, img_7)
    packed_img = call(
        image_end_kernel, packed, pair_specs + [VMEM] * 3, little,
        scale, bias, d_img, img_rows, txt_15, unit, inverse, other_feat,
    )
    other_img = swap(after(packed_img, img_3), 1)
    d_img_feat = dot(packed_img[:, :E], head_weight, 1, 1).astype(BF16)

    parts = call(
        head_kernel, shape(OWNERS, SLABS, 16, 128, dtype=BF16), [SMEM] + [VMEM] * 3,
        4 * ROWS * D * E // 2, core, img_feat, packed_img, other_img,
    )
    parts = after(parts, d_img_feat)
    d_txt = call(
        text_pairs_kernel, block, pair_specs + [VMEM], 2 * pair,
        scale, bias, after(d_txt, parts), txt_rows, other_img, img_3,
    )
    parts = exchange(parts, PLANE)
    slab = (16, 128)
    part = call(sum_kernel, shape(SLABS, *slab, dtype=BF16), [VMEM], little, parts)
    quarters = shape(4, SLABS // 4, *slab, dtype=BF16)
    parts = exchange(after(part, d_txt).reshape(quarters.shape), NEAR)
    parts = call(spread_sum_kernel, quarters, [VMEM], little, parts)
    img_15 = swap(after(img_7, parts), 8)
    parts = exchange(parts, FAR)
    parts = call(spread_sum_kernel, quarters, [VMEM], little, parts)
    parts = exchange(after(parts, img_15), NEAR)
    d_txt_emb = call(
        text_end_kernel, block16, pair_specs + [VMEM] * 2, 4 * pair,
        scale, bias, d_txt, txt_rows, img_7, img_15, txt_emb,
    )
    part = parts.reshape(SLABS, *slab)
    parts = exchange(after(jnp.broadcast_to(part[None], (OWNERS, SLABS, 16, 128))), PLANE)
    d_head = call(
        place_kernel, shape(D, E, dtype=BF16), [SMEM, VMEM, VMEM], 0,
        core, parts, swap(parts, 1),
        scratch=[pltpu.VMEM((D, E), BF16), pltpu.SemaphoreType.DMA((9,))],
        out_specs=pl.BlockSpec(memory_space=pl.ANY),
    )

    return (d_img_feat, d_txt_emb, d_head)


def solution(mesh):
    return jax.shard_map(
        per_device,
        mesh=mesh,
        in_specs=(P("dp", None), P(), P("dp", None), P("dp"), P(), P()),
        out_specs=(P("dp", None), P("dp", None), P()),
        check_vma=False,
    )
```

```python
import jax
import jax.numpy as jnp
from jax import lax
from jax.experimental import pallas as pl
from jax.experimental.pallas import tpu as pltpu
from jax.sharding import PartitionSpec as P

D = 1152
E = 640
ROWS = 256
F32 = jnp.float32
BF16 = jnp.bfloat16
OWNERS, SLABS = 16, 12
SMEM = pl.BlockSpec(memory_space=pltpu.SMEM)
VMEM = pl.BlockSpec(memory_space=pltpu.VMEM)


def group(bits):
    mask = sum(1 << b for b in bits)
    members = [
        sum((k >> j & 1) << b for j, b in enumerate(bits)) for k in range(1 << len(bits))
    ]
    return [[base | m for m in members] for base in range(512) if not base & mask]


PLANE = group((1, 2, 7, 8))
NEAR, FAR = group((3, 4)), group((5, 6))


def swap(value, mask):
    pairs = [(source, source ^ mask) for source in range(lax.axis_size("dp"))]
    return lax.ppermute(value, "dp", pairs)


def exchange(value, members):
    return lax.all_to_all(value, "dp", 0, 0, axis_index_groups=members, tiled=True)


def after(value, *others):
    return lax.optimization_barrier((value,) + others)[0]


def shape(*dims, dtype=F32):
    return jax.ShapeDtypeStruct(dims, dtype)


def dot(left, right, left_dim=1, right_dim=0):
    return lax.dot_general(
        left, right, (((left_dim,), (right_dim,)), ((), ())), preferred_element_type=F32
    )


def call(kernel, out_shape, specs, flops, *operands, scratch=(), out_specs=None):
    moved = sum(x.size * x.dtype.itemsize for x in (*operands, *jax.tree.leaves(out_shape)))
    return pl.pallas_call(
        kernel,
        out_shape=out_shape,
        in_specs=specs,
        out_specs=out_specs if out_specs is not None else jax.tree.map(lambda _: VMEM, out_shape),
        scratch_shapes=scratch,
        compiler_params=pltpu.CompilerParams(vmem_limit_bytes=14 << 20),
        cost_estimate=pl.CostEstimate(flops=flops, bytes_accessed=moved, transcendentals=0),
    )(*operands)


def inverse_norm(value):
    return lax.rsqrt(jnp.sum(value * value, axis=-1, keepdims=True) + 1e-06)


def tangent(d_unit, unit, inverse):
    return ((d_unit - unit * jnp.sum(unit * d_unit, axis=-1, keepdims=True)) * inverse).astype(BF16)


def text_kernel(txt_ref, rows_ref):
    value = txt_ref[...].astype(F32)
    rows_ref[...] = (value * inverse_norm(value)).astype(BF16)


def image_kernel(
    core_ref, scale_ref, bias_ref, labels_ref, feat_ref, head_ref, txt_ref,
    unit_ref, inverse_ref, rows_ref, d_img_ref, d_txt_ref, other_ref,
):
    proj = dot(feat_ref[...], head_ref[...])
    inverse = inverse_norm(proj)
    unit = proj * inverse
    rows = unit.astype(BF16)
    txt = txt_ref[...]
    unit_ref[...] = unit
    inverse_ref[...] = inverse
    rows_ref[...] = rows
    across = jnp.broadcast_to(labels_ref[...].astype(F32), (ROWS, ROWS))
    sign = jnp.where(across == across.T, 1.0, -1.0)
    logits = scale_ref[0] * dot(rows, txt, 1, 1) + bias_ref[0]
    grad = (-sign * jax.nn.sigmoid(-sign * logits)).astype(BF16)
    d_img_ref[...] = dot(grad, txt)
    d_txt_ref[...] = dot(grad, rows, 0, 0)
    other_ref[...] = feat_ref[:, pl.ds(pl.multiple_of(512 * (1 - core_ref[0]), 128), E)]


def pair_term(scale_ref, bias_ref, rows, others):
    logits = scale_ref[0] * dot(rows, others, 1, 1) + bias_ref[0]
    return dot(jax.nn.sigmoid(logits).astype(BF16), others)


def pair_kernel(scale_ref, bias_ref, total_ref, rows_ref, other_ref, out_ref):
    out_ref[...] = total_ref[...] + pair_term(scale_ref, bias_ref, rows_ref[...], other_ref[...])


def image_end_kernel(
    scale_ref, bias_ref, total_ref, rows_ref, other_ref, unit_ref, inverse_ref, feat_ref, packed_ref
):
    rows = rows_ref[...]
    total = total_ref[...] + pair_term(scale_ref, bias_ref, rows, other_ref[...])
    packed_ref[:, :E] = tangent(scale_ref[0] * total, unit_ref[...], inverse_ref[...])
    packed_ref[:, E : 2 * E] = rows
    packed_ref[:, 2 * E :] = feat_ref[...]


def text_first_kernel(scale_ref, bias_ref, total_ref, rows_ref, packed_ref, out_ref):
    term = pair_term(scale_ref, bias_ref, rows_ref[...], packed_ref[:, E : 2 * E])
    out_ref[...] = total_ref[...] + term


def text_pairs_kernel(scale_ref, bias_ref, total_ref, rows_ref, a_ref, b_ref, out_ref):
    rows = rows_ref[...]
    total = total_ref[...] + pair_term(scale_ref, bias_ref, rows, a_ref[...])
    out_ref[...] = total + pair_term(scale_ref, bias_ref, rows, b_ref[...])


def text_end_kernel(scale_ref, bias_ref, total_ref, rows_ref, other_ref, txt_ref, out_ref):
    total = total_ref[...] + pair_term(scale_ref, bias_ref, rows_ref[...], other_ref[...])
    value = txt_ref[...].astype(F32)
    inverse = inverse_norm(value)
    out_ref[...] = tangent(scale_ref[0] * total, value * inverse, inverse)


def sum_kernel(parts_ref, out_ref):
    total = parts_ref[0].astype(F32)
    for k in range(1, parts_ref.shape[0]):
        total = total + parts_ref[k].astype(F32)
    out_ref[...] = total.astype(BF16)


def spread_sum_kernel(parts_ref, out_ref):
    total = parts_ref[0].astype(F32)
    for k in range(1, parts_ref.shape[0]):
        total = total + parts_ref[k].astype(F32)
    out_ref[...] = jnp.broadcast_to(total.astype(BF16)[None], out_ref.shape)


def head_kernel(core_ref, feat_ref, mine_ref, theirs_ref, out_ref):
    core = core_ref[0]
    mine, theirs = mine_ref[:, :E], theirs_ref[:, :E]

    def product(column):
        here = pl.multiple_of(column, 128)
        there = pl.multiple_of(2 * E + column - 512 * core, 128)
        total = dot(feat_ref[:, pl.ds(here, 128)], mine, 0, 0)
        return total + dot(theirs_ref[:, pl.ds(there, 128)], theirs, 0, 0)

    def store(band, rows):
        for t in range(5):
            slab = band * 5 + t
            out_ref[slab // SLABS, slab % SLABS] = rows[:, 128 * t : 128 * t + 128].astype(BF16)

    for block in range(4):
        total = product(5 * 128 * core + 128 * block)
        for j in range(8):
            store(8 * block + j, total[16 * j : 16 * j + 16])
    total = product(512)
    total = jnp.where(core == 0, total[:64], total[64:])
    for j in range(4):
        store(32 + j, total[16 * j : 16 * j + 16])
    out_ref[OWNERS - 1] = jnp.zeros((SLABS, 16, 128), BF16)


def place_kernel(core_ref, mine_ref, theirs_ref, out_ref, whole, sems):
    core = core_ref[0]
    copies = []
    for block in range(9):
        for band in range(8 * block, 8 * block + 8):
            owner = int(band >= 36)
            own = band if band < 36 else band - 40 if band >= 40 else band - 4
            for t in range(5):
                slab = own * 5 + t
                at = (slab // SLABS, slab % SLABS)
                value = jnp.where(core == owner, mine_ref[at], theirs_ref[at])
                whole[16 * band : 16 * band + 16, 128 * t : 128 * t + 128] = value
        rows = pl.ds(128 * block, 128)
        copies.append(pltpu.make_async_copy(whole.at[rows], out_ref.at[rows], sems.at[block]))
        copies[-1].start()
    for copy in copies:
        copy.wait()


def per_device(img_feat, head_weight, txt_emb, labels, log_logit_scale, bias):
    core = (lax.axis_index("dp") & 1)[None]
    scale = jnp.exp(log_logit_scale)
    pair = ROWS * ROWS * E * 4
    little = pair // 100
    block = shape(ROWS, E)
    block16 = shape(ROWS, E, dtype=BF16)

    packed = shape(ROWS, 3 * E, dtype=BF16)
    txt_rows = call(text_kernel, block16, [VMEM], 40 * pair, txt_emb)
    txt_15 = swap(txt_rows, 15)
    unit, inverse, img_rows, d_img, d_txt, other_feat = call(
        image_kernel,
        (block, shape(ROWS, 1), block16, block, block, block16),
        [SMEM, SMEM, SMEM, VMEM, VMEM, VMEM, VMEM],
        12 * pair,
        core, scale, bias, labels[None, :], img_feat, head_weight, txt_rows,
    )
    pair_specs = [SMEM, SMEM, VMEM, VMEM, VMEM]
    late = after(txt_rows, img_rows)
    txt_3, txt_7, txt_1 = swap(late, 3), swap(late, 7), swap(late, 1)
    for other in (txt_15, txt_3, txt_7):
        d_img = call(pair_kernel, block, pair_specs, little, scale, bias, d_img, img_rows, other)
    packed_img = call(
        image_end_kernel, packed, pair_specs + [VMEM] * 3, little,
        scale, bias, d_img, img_rows, txt_1, unit, inverse, other_feat,
    )
    other_img = swap(packed_img, 1)
    d_img_feat = dot(packed_img[:, :E], head_weight, 1, 1).astype(BF16)

    parts = call(
        head_kernel, shape(OWNERS, SLABS, 16, 128, dtype=BF16), [SMEM] + [VMEM] * 3,
        4 * ROWS * D * E // 2, core, img_feat, packed_img, other_img,
    )
    parts = after(parts, d_img_feat)
    late = after(img_rows, parts)
    img_7, img_15, img_3 = swap(late, 7), swap(late, 15), swap(late, 3)
    d_txt = call(
        text_first_kernel, block, pair_specs, pair,
        scale, bias, after(d_txt, parts), txt_rows, other_img,
    )
    parts = exchange(parts, PLANE)
    slab = (16, 128)
    part = call(sum_kernel, shape(SLABS, *slab, dtype=BF16), [VMEM], little, parts)
    part = after(part, d_txt)
    quarters = shape(4, SLABS // 4, *slab, dtype=BF16)
    parts = exchange(part.reshape(quarters.shape), NEAR)
    parts = call(spread_sum_kernel, quarters, [VMEM], little, parts)
    d_txt = call(
        text_pairs_kernel, block, pair_specs + [VMEM], 2 * pair,
        scale, bias, after(d_txt, parts), txt_rows, img_3, img_7,
    )
    parts = after(exchange(parts, FAR), d_txt, img_15)
    parts = call(spread_sum_kernel, quarters, [VMEM], little, parts)
    parts = exchange(parts, NEAR)
    d_txt_emb = call(
        text_end_kernel, block16, pair_specs + [VMEM], pair,
        scale, bias, d_txt, txt_rows, img_15, txt_emb,
    )
    part = parts.reshape(SLABS, *slab)
    parts = exchange(after(jnp.broadcast_to(part[None], (OWNERS, SLABS, 16, 128))), PLANE)
    d_head = call(
        place_kernel, shape(D, E, dtype=BF16), [SMEM, VMEM, VMEM], 0,
        core, parts, swap(parts, 1),
        scratch=[pltpu.VMEM((D, E), BF16), pltpu.SemaphoreType.DMA((9,))],
        out_specs=pl.BlockSpec(memory_space=pl.ANY),
    )

    return (d_img_feat, d_txt_emb, d_head)


def solution(mesh):
    return jax.shard_map(
        per_device,
        mesh=mesh,
        in_specs=(P("dp", None), P(), P("dp", None), P("dp"), P(), P()),
        out_specs=(P("dp", None), P("dp", None), P()),
        check_vma=False,
    )
```

```python
import jax
import jax.numpy as jnp
from jax import lax
from jax.experimental import pallas as pl
from jax.experimental.pallas import tpu as pltpu
from jax.sharding import PartitionSpec as P

D = 1152
E = 640
ROWS = 256
F32 = jnp.float32
BF16 = jnp.bfloat16
OWNERS, SLABS = 16, 12
SMEM = pl.BlockSpec(memory_space=pltpu.SMEM)
VMEM = pl.BlockSpec(memory_space=pltpu.VMEM)


def group(bits):
    mask = sum(1 << b for b in bits)
    members = [
        sum((k >> j & 1) << b for j, b in enumerate(bits)) for k in range(1 << len(bits))
    ]
    return [[base | m for m in members] for base in range(512) if not base & mask]


PLANE = group((1, 2, 7, 8))
LINE = group((3, 4, 5, 6))


def swap(value, mask):
    pairs = [(source, source ^ mask) for source in range(lax.axis_size("dp"))]
    return lax.ppermute(value, "dp", pairs)


def exchange(value, members):
    return lax.all_to_all(value, "dp", 0, 0, axis_index_groups=members, tiled=True)


def after(value, *others):
    return lax.optimization_barrier((value,) + others)[0]


def shape(*dims, dtype=F32):
    return jax.ShapeDtypeStruct(dims, dtype)


def dot(left, right, left_dim=1, right_dim=0):
    return lax.dot_general(
        left, right, (((left_dim,), (right_dim,)), ((), ())), preferred_element_type=F32
    )


def call(kernel, out_shape, specs, flops, *operands, scratch=(), out_specs=None):
    moved = sum(x.size * x.dtype.itemsize for x in (*operands, *jax.tree.leaves(out_shape)))
    return pl.pallas_call(
        kernel,
        out_shape=out_shape,
        in_specs=specs,
        out_specs=out_specs if out_specs is not None else jax.tree.map(lambda _: VMEM, out_shape),
        scratch_shapes=scratch,
        compiler_params=pltpu.CompilerParams(vmem_limit_bytes=14 << 20),
        cost_estimate=pl.CostEstimate(flops=flops, bytes_accessed=moved, transcendentals=0),
    )(*operands)


def inverse_norm(value):
    return lax.rsqrt(jnp.sum(value * value, axis=-1, keepdims=True) + 1e-06)


def tangent(d_unit, unit, inverse):
    return ((d_unit - unit * jnp.sum(unit * d_unit, axis=-1, keepdims=True)) * inverse).astype(BF16)


def text_kernel(txt_ref, rows_ref):
    value = txt_ref[...].astype(F32)
    rows_ref[...] = (value * inverse_norm(value)).astype(BF16)


def image_kernel(
    core_ref, scale_ref, bias_ref, labels_ref, feat_ref, head_ref, txt_ref,
    unit_ref, inverse_ref, rows_ref, d_img_ref, d_txt_ref, other_ref,
):
    proj = dot(feat_ref[...], head_ref[...])
    inverse = inverse_norm(proj)
    unit = proj * inverse
    rows = unit.astype(BF16)
    txt = txt_ref[...]
    unit_ref[...] = unit
    inverse_ref[...] = inverse
    rows_ref[...] = rows
    across = jnp.broadcast_to(labels_ref[...].astype(F32), (ROWS, ROWS))
    sign = jnp.where(across == across.T, 1.0, -1.0)
    logits = scale_ref[0] * dot(rows, txt, 1, 1) + bias_ref[0]
    grad = (-sign * jax.nn.sigmoid(-sign * logits)).astype(BF16)
    d_img_ref[...] = dot(grad, txt)
    d_txt_ref[...] = dot(grad, rows, 0, 0)
    other_ref[...] = feat_ref[:, pl.ds(pl.multiple_of(512 * (1 - core_ref[0]), 128), E)]


def pair_term(scale_ref, bias_ref, rows, others):
    logits = scale_ref[0] * dot(rows, others, 1, 1) + bias_ref[0]
    return dot(jax.nn.sigmoid(logits).astype(BF16), others)


def pair_kernel(scale_ref, bias_ref, total_ref, rows_ref, other_ref, out_ref):
    out_ref[...] = total_ref[...] + pair_term(scale_ref, bias_ref, rows_ref[...], other_ref[...])


def image_end_kernel(
    scale_ref, bias_ref, total_ref, rows_ref, a_ref, b_ref, unit_ref, inverse_ref, feat_ref, packed_ref
):
    rows = rows_ref[...]
    total = total_ref[...] + pair_term(scale_ref, bias_ref, rows, a_ref[...])
    total = total + pair_term(scale_ref, bias_ref, rows, b_ref[...])
    packed_ref[:, :E] = tangent(scale_ref[0] * total, unit_ref[...], inverse_ref[...])
    packed_ref[:, E : 2 * E] = rows
    packed_ref[:, 2 * E :] = feat_ref[...]


def text_pairs_kernel(scale_ref, bias_ref, total_ref, rows_ref, packed_ref, a_ref, b_ref, out_ref):
    rows = rows_ref[...]
    total = total_ref[...] + pair_term(scale_ref, bias_ref, rows, packed_ref[:, E : 2 * E])
    total = total + pair_term(scale_ref, bias_ref, rows, a_ref[...])
    out_ref[...] = total + pair_term(scale_ref, bias_ref, rows, b_ref[...])


def text_end_kernel(scale_ref, bias_ref, total_ref, rows_ref, other_ref, txt_ref, out_ref):
    total = total_ref[...] + pair_term(scale_ref, bias_ref, rows_ref[...], other_ref[...])
    value = txt_ref[...].astype(F32)
    inverse = inverse_norm(value)
    out_ref[...] = tangent(scale_ref[0] * total, value * inverse, inverse)


def plane_sum_kernel(parts_ref, out_ref):
    total = parts_ref[0].astype(F32)
    for k in range(1, parts_ref.shape[0]):
        total = total + parts_ref[k].astype(F32)
    out_ref[:SLABS] = total.astype(BF16)
    out_ref[SLABS:] = jnp.zeros((OWNERS - SLABS, 16, 128), BF16)


def spread_sum_kernel(parts_ref, out_ref):
    total = parts_ref[0].astype(F32)
    for k in range(1, parts_ref.shape[0]):
        total = total + parts_ref[k].astype(F32)
    out_ref[...] = jnp.broadcast_to(total.astype(BF16)[None], out_ref.shape)


def head_kernel(core_ref, feat_ref, mine_ref, theirs_ref, out_ref):
    core = core_ref[0]
    mine, theirs = mine_ref[:, :E], theirs_ref[:, :E]

    def product(column):
        here = pl.multiple_of(column, 128)
        there = pl.multiple_of(2 * E + column - 512 * core, 128)
        total = dot(feat_ref[:, pl.ds(here, 128)], mine, 0, 0)
        return total + dot(theirs_ref[:, pl.ds(there, 128)], theirs, 0, 0)

    def store(band, rows):
        for t in range(5):
            slab = band * 5 + t
            out_ref[slab // SLABS, slab % SLABS] = rows[:, 128 * t : 128 * t + 128].astype(BF16)

    for block in range(4):
        total = product(5 * 128 * core + 128 * block)
        for j in range(8):
            store(8 * block + j, total[16 * j : 16 * j + 16])
    total = product(512)
    total = jnp.where(core == 0, total[:64], total[64:])
    for j in range(4):
        store(32 + j, total[16 * j : 16 * j + 16])
    out_ref[OWNERS - 1] = jnp.zeros((SLABS, 16, 128), BF16)


def place_kernel(core_ref, mine_ref, theirs_ref, out_ref, whole, sems):
    core = core_ref[0]
    copies = []
    for block in range(9):
        for band in range(8 * block, 8 * block + 8):
            owner = int(band >= 36)
            own = band if band < 36 else band - 40 if band >= 40 else band - 4
            for t in range(5):
                slab = own * 5 + t
                at = (slab // SLABS, slab % SLABS)
                value = jnp.where(core == owner, mine_ref[at], theirs_ref[at])
                whole[16 * band : 16 * band + 16, 128 * t : 128 * t + 128] = value
        rows = pl.ds(128 * block, 128)
        copies.append(pltpu.make_async_copy(whole.at[rows], out_ref.at[rows], sems.at[block]))
        copies[-1].start()
    for copy in copies:
        copy.wait()


def per_device(img_feat, head_weight, txt_emb, labels, log_logit_scale, bias):
    core = (lax.axis_index("dp") & 1)[None]
    scale = jnp.exp(log_logit_scale)
    pair = ROWS * ROWS * E * 4
    little = pair // 100
    block = shape(ROWS, E)
    block16 = shape(ROWS, E, dtype=BF16)

    packed = shape(ROWS, 3 * E, dtype=BF16)
    txt_rows = call(text_kernel, block16, [VMEM], little, txt_emb)
    txt_15, txt_3, txt_7, txt_1 = [swap(txt_rows, c) for c in (15, 3, 7, 1)]
    unit, inverse, img_rows, d_img, d_txt, other_feat = call(
        image_kernel,
        (block, shape(ROWS, 1), block16, block, block, block16),
        [SMEM, SMEM, SMEM, VMEM, VMEM, VMEM, VMEM],
        12 * pair,
        core, scale, bias, labels[None, :], img_feat, head_weight, txt_rows,
    )
    pair_specs = [SMEM, SMEM, VMEM, VMEM, VMEM]
    for other in (txt_15, txt_3):
        d_img = call(pair_kernel, block, pair_specs, little, scale, bias, d_img, img_rows, other)
    packed_img = call(
        image_end_kernel, packed, pair_specs + [VMEM] * 4, little,
        scale, bias, d_img, img_rows, txt_7, txt_1, unit, inverse, other_feat,
    )
    other_img = swap(packed_img, 1)
    d_img_feat = dot(packed_img[:, :E], head_weight, 1, 1).astype(BF16)

    parts = call(
        head_kernel, shape(OWNERS, SLABS, 16, 128, dtype=BF16), [SMEM] + [VMEM] * 3,
        4 * ROWS * D * E // 2, core, img_feat, packed_img, other_img,
    )
    parts = after(parts, d_img_feat)
    late = after(img_rows, parts)
    img_7, img_15, img_3 = swap(late, 7), swap(late, 15), swap(late, 3)
    parts = exchange(parts, PLANE)
    slab = (16, 128)
    line = shape(OWNERS, *slab, dtype=BF16)
    parts = call(plane_sum_kernel, line, [VMEM], little, parts)
    d_txt = call(
        text_pairs_kernel, block, pair_specs + [VMEM] * 2, 3 * pair,
        scale, bias, after(d_txt, parts), txt_rows, other_img, img_3, img_7,
    )
    parts = after(exchange(parts, LINE), d_txt, img_15)
    parts = call(spread_sum_kernel, line, [VMEM], little, parts)
    parts = exchange(parts, LINE)[:SLABS]
    d_txt_emb = call(
        text_end_kernel, block16, pair_specs + [VMEM], pair,
        scale, bias, d_txt, txt_rows, img_15, txt_emb,
    )
    part = parts.reshape(SLABS, *slab)
    parts = exchange(after(jnp.broadcast_to(part[None], (OWNERS, SLABS, 16, 128))), PLANE)
    d_head = call(
        place_kernel, shape(D, E, dtype=BF16), [SMEM, VMEM, VMEM], 0,
        core, parts, swap(parts, 1),
        scratch=[pltpu.VMEM((D, E), BF16), pltpu.SemaphoreType.DMA((9,))],
        out_specs=pl.BlockSpec(memory_space=pl.ANY),
    )

    return (d_img_feat, d_txt_emb, d_head)


def solution(mesh):
    return jax.shard_map(
        per_device,
        mesh=mesh,
        in_specs=(P("dp", None), P(), P("dp", None), P("dp"), P(), P()),
        out_specs=(P("dp", None), P("dp", None), P()),
        check_vma=False,
    )
```

```python
import jax
import jax.numpy as jnp
from jax import lax
from jax.experimental import pallas as pl
from jax.experimental.pallas import tpu as pltpu
from jax.sharding import PartitionSpec as P

D = 1152
E = 640
ROWS = 256
F32 = jnp.float32
BF16 = jnp.bfloat16
OWNERS, SLABS = 16, 12
SMEM = pl.BlockSpec(memory_space=pltpu.SMEM)
VMEM = pl.BlockSpec(memory_space=pltpu.VMEM)


def group(bits):
    mask = sum(1 << b for b in bits)
    members = [
        sum((k >> j & 1) << b for j, b in enumerate(bits)) for k in range(1 << len(bits))
    ]
    return [[base | m for m in members] for base in range(512) if not base & mask]


PLANE = group((1, 2, 7, 8))
LINE = group((3, 4, 5, 6))


def swap(value, mask):
    pairs = [(source, source ^ mask) for source in range(lax.axis_size("dp"))]
    return lax.ppermute(value, "dp", pairs)


def exchange(value, members):
    return lax.all_to_all(value, "dp", 0, 0, axis_index_groups=members, tiled=True)


def after(value, *others):
    return lax.optimization_barrier((value,) + others)[0]


def shape(*dims, dtype=F32):
    return jax.ShapeDtypeStruct(dims, dtype)


def dot(left, right, left_dim=1, right_dim=0):
    return lax.dot_general(
        left, right, (((left_dim,), (right_dim,)), ((), ())), preferred_element_type=F32
    )


def call(kernel, out_shape, specs, flops, *operands, scratch=(), out_specs=None):
    moved = sum(x.size * x.dtype.itemsize for x in (*operands, *jax.tree.leaves(out_shape)))
    return pl.pallas_call(
        kernel,
        out_shape=out_shape,
        in_specs=specs,
        out_specs=out_specs if out_specs is not None else jax.tree.map(lambda _: VMEM, out_shape),
        scratch_shapes=scratch,
        compiler_params=pltpu.CompilerParams(vmem_limit_bytes=14 << 20),
        cost_estimate=pl.CostEstimate(flops=flops, bytes_accessed=moved, transcendentals=0),
    )(*operands)


def inverse_norm(value):
    return lax.rsqrt(jnp.sum(value * value, axis=-1, keepdims=True) + 1e-06)


def tangent(d_unit, unit, inverse):
    return ((d_unit - unit * jnp.sum(unit * d_unit, axis=-1, keepdims=True)) * inverse).astype(BF16)


def unit_rows(ref):
    value = ref[...].astype(F32)
    return (value * inverse_norm(value)).astype(BF16)


def text_kernel(txt_ref, rows_ref):
    rows_ref[...] = unit_rows(txt_ref)


def image_kernel(
    core_ref, scale_ref, bias_ref, labels_ref, feat_ref, head_ref, txt_ref,
    unit_ref, inverse_ref, rows_ref, d_img_ref, d_txt_ref, other_ref,
):
    proj = dot(feat_ref[...], head_ref[...])
    inverse = inverse_norm(proj)
    unit = proj * inverse
    rows = unit.astype(BF16)
    txt = txt_ref[...]
    unit_ref[...] = unit
    inverse_ref[...] = inverse
    rows_ref[...] = rows
    across = jnp.broadcast_to(labels_ref[...].astype(F32), (ROWS, ROWS))
    sign = jnp.where(across == across.T, 1.0, -1.0)
    logits = scale_ref[0] * dot(rows, txt, 1, 1) + bias_ref[0]
    grad = (-sign * jax.nn.sigmoid(-sign * logits)).astype(BF16)
    d_img_ref[...] = dot(grad, txt)
    d_txt_ref[...] = dot(grad, rows, 0, 0)
    other_ref[...] = feat_ref[:, pl.ds(pl.multiple_of(512 * (1 - core_ref[0]), 128), E)]


def pair_term(scale_ref, bias_ref, rows, others):
    logits = scale_ref[0] * dot(rows, others, 1, 1) + bias_ref[0]
    return dot(jax.nn.sigmoid(logits).astype(BF16), others)


def three_pairs_kernel(
    scale_ref, bias_ref, total_ref, rows_ref, a_ref, b_ref, c_ref, out_ref, held, sems
):
    copies = [
        pltpu.make_async_copy(ref, held.at[k], sems.at[k])
        for k, ref in enumerate((a_ref, b_ref, c_ref))
    ]
    for copy in copies:
        copy.start()
    rows, total = rows_ref[...], total_ref[...]
    for k, copy in enumerate(copies):
        copy.wait()
        total = total + pair_term(scale_ref, bias_ref, rows, unit_rows(held.at[k]))
    out_ref[...] = total


def image_end_kernel(
    scale_ref, bias_ref, total_ref, rows_ref, other_ref, unit_ref, inverse_ref, feat_ref, packed_ref
):
    rows = rows_ref[...]
    total = total_ref[...] + pair_term(scale_ref, bias_ref, rows, unit_rows(other_ref))
    packed_ref[:, :E] = tangent(scale_ref[0] * total, unit_ref[...], inverse_ref[...])
    packed_ref[:, E : 2 * E] = rows
    packed_ref[:, 2 * E :] = feat_ref[...]


def text_pairs_kernel(scale_ref, bias_ref, total_ref, rows_ref, a_ref, b_ref, out_ref):
    rows = rows_ref[...]
    total = total_ref[...] + pair_term(scale_ref, bias_ref, rows, a_ref[...])
    out_ref[...] = total + pair_term(scale_ref, bias_ref, rows, b_ref[...])


def text_end_kernel(
    scale_ref, bias_ref, total_ref, rows_ref, packed_ref, other_ref, txt_ref, out_ref
):
    rows = rows_ref[...]
    total = total_ref[...] + pair_term(scale_ref, bias_ref, rows, packed_ref[:, E : 2 * E])
    total = total + pair_term(scale_ref, bias_ref, rows, other_ref[...])
    value = txt_ref[...].astype(F32)
    inverse = inverse_norm(value)
    out_ref[...] = tangent(scale_ref[0] * total, value * inverse, inverse)


def plane_sum_kernel(parts_ref, out_ref):
    total = parts_ref[0].astype(F32)
    for k in range(1, parts_ref.shape[0]):
        total = total + parts_ref[k].astype(F32)
    out_ref[:SLABS] = total.astype(BF16)
    out_ref[SLABS:] = jnp.zeros((OWNERS - SLABS, 16, 128), BF16)


def spread_sum_kernel(parts_ref, out_ref):
    total = parts_ref[0].astype(F32)
    for k in range(1, parts_ref.shape[0]):
        total = total + parts_ref[k].astype(F32)
    out_ref[...] = jnp.broadcast_to(total.astype(BF16)[None], out_ref.shape)


def head_kernel(core_ref, feat_ref, mine_ref, theirs_ref, out_ref):
    core = core_ref[0]
    mine, theirs = mine_ref[:, :E], theirs_ref[:, :E]

    def product(column):
        here = pl.multiple_of(column, 128)
        there = pl.multiple_of(2 * E + column - 512 * core, 128)
        total = dot(feat_ref[:, pl.ds(here, 128)], mine, 0, 0)
        return total + dot(theirs_ref[:, pl.ds(there, 128)], theirs, 0, 0)

    def store(band, rows):
        for t in range(5):
            slab = band * 5 + t
            out_ref[slab // SLABS, slab % SLABS] = rows[:, 128 * t : 128 * t + 128].astype(BF16)

    for block in range(4):
        total = product(5 * 128 * core + 128 * block)
        for j in range(8):
            store(8 * block + j, total[16 * j : 16 * j + 16])
    total = product(512)
    total = jnp.where(core == 0, total[:64], total[64:])
    for j in range(4):
        store(32 + j, total[16 * j : 16 * j + 16])
    out_ref[OWNERS - 1] = jnp.zeros((SLABS, 16, 128), BF16)


def place_kernel(core_ref, mine_ref, theirs_ref, out_ref, whole, sems):
    core = core_ref[0]
    copies = []
    for block in range(9):
        for band in range(8 * block, 8 * block + 8):
            owner = int(band >= 36)
            own = band if band < 36 else band - 40 if band >= 40 else band - 4
            for t in range(5):
                slab = own * 5 + t
                at = (slab // SLABS, slab % SLABS)
                value = jnp.where(core == owner, mine_ref[at], theirs_ref[at])
                whole[16 * band : 16 * band + 16, 128 * t : 128 * t + 128] = value
        rows = pl.ds(128 * block, 128)
        copies.append(pltpu.make_async_copy(whole.at[rows], out_ref.at[rows], sems.at[block]))
        copies[-1].start()
    for copy in copies:
        copy.wait()


def per_device(img_feat, head_weight, txt_emb, labels, log_logit_scale, bias):
    core = (lax.axis_index("dp") & 1)[None]
    scale = jnp.exp(log_logit_scale)
    pair = ROWS * ROWS * E * 4
    little = pair // 100
    block = shape(ROWS, E)
    block16 = shape(ROWS, E, dtype=BF16)

    packed = shape(ROWS, 3 * E, dtype=BF16)
    txt_15, txt_3, txt_1, txt_7 = [swap(txt_emb, c) for c in (15, 3, 1, 7)]
    txt_rows = call(text_kernel, block16, [VMEM], 12 * pair, txt_emb)
    unit, inverse, img_rows, d_img, d_txt, other_feat = call(
        image_kernel,
        (block, shape(ROWS, 1), block16, block, block, block16),
        [SMEM, SMEM, SMEM, VMEM, VMEM, VMEM, VMEM],
        12 * pair,
        core, scale, bias, labels[None, :], img_feat, head_weight, txt_rows,
    )
    pair_specs = [SMEM, SMEM, VMEM, VMEM, VMEM]
    d_img = call(
        three_pairs_kernel, block, pair_specs[:4] + [pl.BlockSpec(memory_space=pl.ANY)] * 3, little,
        scale, bias, d_img, img_rows, txt_15, txt_3, txt_1,
        scratch=[pltpu.VMEM((3, ROWS, E), BF16), pltpu.SemaphoreType.DMA((3,))],
    )
    packed_img = call(
        image_end_kernel, packed, pair_specs + [VMEM] * 3, little,
        scale, bias, d_img, img_rows, txt_7, unit, inverse, other_feat,
    )
    other_img = swap(packed_img, 1)
    d_img_feat = dot(packed_img[:, :E], head_weight, 1, 1).astype(BF16)

    parts = call(
        head_kernel, shape(OWNERS, SLABS, 16, 128, dtype=BF16), [SMEM] + [VMEM] * 3,
        4 * ROWS * D * E // 2, core, img_feat, packed_img, other_img,
    )
    parts = after(parts, d_img_feat)
    late = after(img_rows, parts)
    img_7, img_15, img_3 = swap(late, 7), swap(late, 15), swap(late, 3)
    parts = exchange(parts, PLANE)
    slab = (16, 128)
    line = shape(OWNERS, *slab, dtype=BF16)
    parts = call(plane_sum_kernel, line, [VMEM], little, parts)
    d_txt = call(
        text_pairs_kernel, block, pair_specs + [VMEM], 2 * pair,
        scale, bias, after(d_txt, parts), txt_rows, img_3, img_7,
    )
    parts = after(exchange(parts, LINE), d_txt, img_15)
    parts = call(spread_sum_kernel, line, [VMEM], little, parts)
    parts = exchange(parts, LINE)[:SLABS]
    d_txt_emb = call(
        text_end_kernel, block16, pair_specs + [VMEM] * 2, 2 * pair,
        scale, bias, d_txt, txt_rows, other_img, img_15, txt_emb,
    )
    part = parts.reshape(SLABS, *slab)
    parts = exchange(after(jnp.broadcast_to(part[None], (OWNERS, SLABS, 16, 128))), PLANE)
    d_head = call(
        place_kernel, shape(D, E, dtype=BF16), [SMEM, VMEM, VMEM], 0,
        core, parts, swap(parts, 1),
        scratch=[pltpu.VMEM((D, E), BF16), pltpu.SemaphoreType.DMA((9,))],
        out_specs=pl.BlockSpec(memory_space=pl.ANY),
    )

    return (d_img_feat, d_txt_emb, d_head)


def solution(mesh):
    return jax.shard_map(
        per_device,
        mesh=mesh,
        in_specs=(P("dp", None), P(), P("dp", None), P("dp"), P(), P()),
        out_specs=(P("dp", None), P("dp", None), P()),
        check_vma=False,
    )
```
